32 devices in a mesh: path: 8 (over z, y), fsdp: 4 (over x, core).
Axes of the slice: x: 2, y: 2, z: 4, core: 2. Of those that a mesh axis runs over, the one named last changes fastest.
Arguments:
- tokens: bfloat16 [8, 1024, 4096], P('path', 'fsdp'), may hold values from -6 to 6
- cotangent: bfloat16 [8, 1024, 256], P('path', 'fsdp'), may hold values from -6 to 6
- module_table: int32 [8, 1], replicated, may hold values from 0 to 7
- module_weights: bfloat16 [8, 4096, 256], P(None, 'fsdp'), may hold values from -6 to 6
- momentum: float32 [8, 4096, 256], P(None, 'fsdp'), may hold values from -6 to 6
Outputs:
- new_weights: bfloat16 [8, 4096, 256], P(None, 'fsdp')
- new_momentum: float32 [8, 4096, 256], P(None, 'fsdp')
The draws below stay inside these ranges and needn't reach their ends.
Inputs may be any that keep to these rules, and one draw needn't show every extreme that they name: `module_table`: every module is taken by at least one path.
All inputs are finite; a program needn't handle non-finite values.
Results may differ from the reference program's by a relative error of at most 0.0034.
Values may be sent and summed in bfloat16 or wider, within the bound.
No kernel may reach another device: no remote copies, remote signals or barrier semaphores. Data moves between devices by JAX's collectives and lax.ppermute only.
A program may use at most 64 MiB of HBM per device.

```python
import math
import jax
import jax.numpy as jnp
from jax import lax

D = 4096
R = 256
MODS = 8
PATHS = 8
PATH_TOKENS = 1024


def block_scale(stream_key, extent, shards, low, largest):
    level, own = 1.0, jax.random.fold_in(stream_key, 6)
    for dim, shards_of in shards:
        draws = jnp.exp(jax.random.uniform(jax.random.fold_in(own, dim), (shards_of,), jnp.float32, low / len(shards), largest / len(shards)))
        level = level * jnp.repeat(draws, extent[dim] // shards_of).reshape([-1 if axis == dim else 1 for axis in range(len(extent))])
    return level


def different_ones(key, rows, count, top, lift):
    ranking = jax.random.permutation(jax.random.fold_in(key, 1), count)
    boost = ranking
    for power in range(3):
        boost = boost * boost // count
    boost = boost * lift // count
    chance = jax.random.randint(jax.random.fold_in(key, 2), (rows, count), 0, 4096) + boost
    fixed_rows = jax.random.permutation(jax.random.fold_in(key, 3), rows)[jnp.arange(count) % rows]
    chance = jnp.where(jnp.arange(rows)[:, None] == fixed_rows[None, :], 1 << 14, chance)
    merit = chance * count + jnp.arange(count)
    return lax.top_k(merit.astype(jnp.int32), top)[1].astype(jnp.int32)


def scatter_about(own_key, dims, deviation, bound, shards=(), kind=jnp.bfloat16):
    drawn = jax.random.normal(own_key, dims, jnp.float32) * deviation
    if len(shards) > 0:
        drawn = block_scale(own_key, dims, shards, -0.22, 0.18) * drawn
    return jnp.clip(drawn, min=-bound, max=bound).astype(kind)


def setup_inputs(seed: int = 0) -> dict:
    key_list = jax.random.split(jax.random.key(seed), 6)
    return {
        "tokens": scatter_about(key_list[0], (PATHS, PATH_TOKENS, D), 1.0, 6.0, ((0, 8), (1, 4))),
        "cotangent": scatter_about(key_list[1], (PATHS, PATH_TOKENS, R), 1.0, 6.0, ((0, 8), (1, 4))),
        "module_table": different_ones(key_list[2], PATHS, MODS, 1, 2048),
        "module_weights": scatter_about(key_list[3], (MODS, D, R), 1.0, 6.0, ((1, 4),)),
        "momentum": scatter_about(key_list[4], (MODS, D, R), 1.0, 6.0, ((1, 4),), jnp.float32),
    }


def path_delta(path_rows, path_cotangent, weights, step_size):
    latent = jnp.dot(path_rows, weights, preferred_element_type=jnp.float32)
    inverse_rms = lax.rsqrt(lax.optimization_barrier(jnp.mean(latent * latent, axis=-1, keepdims=True)) + 1e-06)
    normed = latent * inverse_rms
    upstream = path_cotangent.astype(jnp.float32)
    latent_cotangent = (inverse_rms * (upstream - normed * lax.optimization_barrier(jnp.mean(upstream * normed, axis=-1, keepdims=True)))).astype(jnp.bfloat16)
    gradient = lax.dot_general(path_rows, latent_cotangent, (((0,), (0,)), ((), ())), preferred_element_type=jnp.float32)
    return gradient * step_size

def reference(tokens, cotangent, module_table, module_weights, momentum):
    module_count = module_weights.shape[0]
    step_size = math.sqrt(D / PATH_TOKENS)
    choices_col = module_table[:, 0].astype(jnp.int32)
    module_ids = jnp.arange(module_count, dtype=jnp.int32)

    def accumulate(sums, items):
        path_rows, path_cotangent, module = items
        weights = lax.dynamic_index_in_dim(module_weights, module, 0, keepdims=False)
        delta = path_delta(path_rows, path_cotangent, weights, step_size)
        picked = (module_ids == module).astype(sums.dtype)
        return (sums + picked[:, None, None] * delta[None], None)
    start_sums = jnp.zeros(module_weights.shape, jnp.float32)
    sums, unused = lax.scan(accumulate, start_sums, (tokens, cotangent, choices_col))
    counts = lax.optimization_barrier(jnp.sum((choices_col[:, None] == module_ids[None, :]).astype(jnp.float32), axis=0))
    average = sums / counts[:, None, None]
    new_momentum = 0.9 * momentum + average
    new_weights = (module_weights.astype(jnp.float32) - 0.7 * (average + 0.9 * new_momentum)).astype(jnp.bfloat16)
    return (new_weights, new_momentum)
```

```python
import math

import jax
import jax.numpy as jnp
import numpy as np
from jax import lax
from jax.experimental import pallas as pl
from jax.experimental.pallas import tpu as pltpu
from jax.sharding import PartitionSpec as P

CHAINS = 2


def outer_update(weights, moment, average):
    new_moment = 0.9 * moment + average
    new_weights = (weights.astype(jnp.float32) - 0.7 * (average + 0.9 * new_moment)).astype(
        jnp.bfloat16
    )
    return (new_weights, new_moment)


def ring_order(paths):
    return [p for p in range(0, paths, 2)] + [p for p in range(paths - 1, 0, -2)]


def ring_plan(paths, shards):
    order = ring_order(paths)
    place = {p: i for i, p in enumerate(order)}
    pairs = []
    source = np.zeros((paths, 2, paths), np.int32)
    for p in range(paths):
        for f in range(shards):
            way = 1 if f % 2 == 0 else -1
            pairs.append((p * shards + f, order[(place[p] + way) % paths] * shards + f))
        for core in range(2):
            way = 1 if core == 0 else -1
            for step in range(paths):
                source[p, core, step] = order[(place[p] - way * step) % paths]
    return pairs, source


def apply_kernel(index_ref, block_ref, weights_ref, moment_ref, *rest):
    new_weights_ref, new_moment_ref = rest[-2:]
    average = block_ref[...].astype(jnp.float32)
    new_weights, new_moment = outer_update(weights_ref[0], moment_ref[0], average)
    new_weights_ref[0] = new_weights
    new_moment_ref[0] = new_moment


def apply_block(modules, step, chain, block, weights, moment, outs):
    rows, width = block.shape
    tile = min(rows, 256)
    tiles = rows // tile

    def spot(i, index):
        return (index[0], chain * tiles + i, 0)

    module = lax.dynamic_slice_in_dim(modules, step, 1)
    spec = pl.BlockSpec((1, tile, width), spot)
    in_specs = [pl.BlockSpec((tile, width), lambda i, index: (i, 0)), spec, spec]
    args = [block, weights, moment]
    aliases = {}
    if outs is not None:
        in_specs += [pl.BlockSpec(memory_space=pl.ANY)] * 2
        args += list(outs)
        aliases = {4: 0, 5: 1}
    return pl.pallas_call(
        apply_kernel,
        grid_spec=pltpu.PrefetchScalarGridSpec(
            num_scalar_prefetch=1, grid=(tiles,), in_specs=in_specs, out_specs=[spec, spec]
        ),
        out_shape=[
            jax.ShapeDtypeStruct(weights.shape, weights.dtype),
            jax.ShapeDtypeStruct(moment.shape, moment.dtype),
        ],
        input_output_aliases=aliases,
        cost_estimate=pl.CostEstimate(
            flops=6 * rows * width, bytes_accessed=14 * rows * width, transcendentals=0
        ),
        name="apply_block",
    )(module, *args)


def body(tokens, cotangent, module_table, module_weights, momentum):
    paths, shards = lax.axis_size("path"), lax.axis_size("fsdp")
    chips = shards // 2
    path_id, shard_id = lax.axis_index("path"), lax.axis_index("fsdp")
    core, chip = shard_id % 2, shard_id // 2
    tok_rows, width = tokens.shape[1:]
    module_count, rows, features = module_weights.shape
    step_size = math.sqrt(width / (tok_rows * shards))
    choices = module_table[:, 0]
    module = lax.dynamic_index_in_dim(choices, path_id, 0, keepdims=False)

    to_core = [(i, i ^ 1) for i in range(shards)]

    def to_chip(step):
        return [(i, (i + 2 * step) % shards) for i in range(shards)]

    own_weights = lax.dynamic_index_in_dim(module_weights, module, 0, keepdims=False)
    blocks = [own_weights] + [
        lax.ppermute(own_weights, "fsdp", to_chip(s)) for s in range(1, chips)
    ]
    split = tokens[0].reshape(tok_rows, chips, 2, rows)
    kept = lax.dynamic_index_in_dim(split, core, 2, keepdims=False)
    given = lax.dynamic_index_in_dim(split, 1 - core, 2, keepdims=False)
    taken = lax.ppermute(given, "fsdp", to_core)
    first = core == 0
    columns = jnp.where(
        first, jnp.concatenate([kept, taken]), jnp.concatenate([taken, kept])
    )
    other_up = lax.ppermute(cotangent[0], "fsdp", to_core)
    upstream = jnp.where(
        first,
        jnp.concatenate([cotangent[0], other_up]),
        jnp.concatenate([other_up, cotangent[0]]),
    ).astype(jnp.float32)

    def chip_columns(index):
        return lax.dynamic_index_in_dim(columns, index, 1, keepdims=False)

    partial = sum(
        jnp.dot(
            chip_columns((chip - s) % chips), blocks[s], preferred_element_type=jnp.float32
        )
        for s in range(chips)
    )
    latent = partial + lax.ppermute(partial, "fsdp", to_core)
    inverse_rms = lax.rsqrt(jnp.mean(latent * latent, axis=-1, keepdims=True) + 1e-06)
    normed = latent * inverse_rms
    latent_cotangent = (
        inverse_rms * (upstream - normed * jnp.mean(upstream * normed, axis=-1, keepdims=True))
    ).astype(jnp.bfloat16)

    def gradient(index, chain, chains):
        part = lax.dynamic_slice_in_dim(
            chip_columns(index), chain * (rows // chains), rows // chains, 1
        )
        return lax.dot_general(
            part, latent_cotangent, (((0,), (0,)), ((), ())), preferred_element_type=jnp.float32
        )

    def path_delta(chain, chains):
        total = gradient(chip, chain, chains)
        for s in range(1, chips):
            there = gradient((chip + s) % chips, chain, chains).astype(jnp.bfloat16)
            total = total + lax.ppermute(there, "fsdp", to_chip(s)).astype(jnp.float32)
        return total * step_size

    if paths != module_count:
        module_ids = jnp.arange(module_count, dtype=jnp.int32)
        picked = (module_ids == module).astype(jnp.float32)
        counts = jnp.sum((choices[:, None] == module_ids[None, :]).astype(jnp.float32), axis=0)
        summed = lax.psum(picked[:, None, None] * path_delta(0, 1)[None], "path")
        return outer_update(module_weights, momentum, summed / counts[:, None, None])

    pairs, source = ring_plan(paths, shards)
    sources = jnp.asarray(source).reshape(paths * 2, paths)
    mine = lax.dynamic_index_in_dim(sources, path_id * 2 + core, 0, keepdims=False)
    modules = jnp.sum(
        jnp.where(mine[:, None] == jnp.arange(paths)[None, :], choices[None, :], 0), axis=1
    ).astype(jnp.int32)
    held = [path_delta(c, CHAINS).astype(jnp.bfloat16) for c in range(CHAINS)]
    outs = None
    for step in range(paths):
        for chain in range(CHAINS):
            block = held[chain]
            if step < paths - 1:
                held[chain] = lax.ppermute(block, ("path", "fsdp"), pairs)
            outs = apply_block(modules, step, chain, block, module_weights, momentum, outs)
    return tuple(outs)


def solution(mesh):
    return jax.shard_map(
        body,
        mesh=mesh,
        in_specs=(
            P("path", "fsdp", None),
            P("path", "fsdp", None),
            P(),
            P(None, "fsdp", None),
            P(None, "fsdp", None),
        ),
        out_specs=(P(None, "fsdp", None), P(None, "fsdp", None)),
        check_vma=False,
    )
```

```python
import functools
import math

import jax
import jax.numpy as jnp
import numpy as np
from jax import lax
from jax.experimental import pallas as pl
from jax.experimental.pallas import tpu as pltpu
from jax.sharding import PartitionSpec as P

CHAINS = 2
MIB = 1 << 20
VMEM = pl.BlockSpec(memory_space=pltpu.VMEM)
SMEM = pl.BlockSpec(memory_space=pltpu.SMEM)
ANY = pl.BlockSpec(memory_space=pl.ANY)


def outer_update(weights, moment, average):
    new_moment = 0.9 * moment + average
    new_weights = (weights.astype(jnp.float32) - 0.7 * (average + 0.9 * new_moment)).astype(
        jnp.bfloat16
    )
    return (new_weights, new_moment)


def ring_order(paths):
    return [p for p in range(0, paths, 2)] + [p for p in range(paths - 1, 0, -2)]


def ring_plan(paths, shards):
    order = ring_order(paths)
    place = {p: i for i, p in enumerate(order)}
    pairs = []
    source = np.zeros((paths, 2, paths), np.int32)
    for p in range(paths):
        for f in range(shards):
            way = 1 if f % 2 == 0 else -1
            pairs.append((p * shards + f, order[(place[p] + way) % paths] * shards + f))
        for core in range(2):
            way = 1 if core == 0 else -1
            for step in range(paths):
                source[p, core, step] = order[(place[p] - way * step) % paths]
    return pairs, source


def call(kernel, out_shape, in_specs, out_specs, args, scratch=(), limit=8, cost=None):
    return pl.pallas_call(
        kernel,
        in_specs=in_specs,
        out_specs=out_specs,
        out_shape=out_shape,
        scratch_shapes=list(scratch),
        compiler_params=pltpu.CompilerParams(vmem_limit_bytes=limit * MIB),
        cost_estimate=cost,
        name=kernel.func.__name__ if isinstance(kernel, functools.partial) else kernel.__name__,
    )(*args)


def pick_rows(table_ref, where_ref, weights_ref, out_ref, sem):
    copy = pltpu.make_async_copy(weights_ref.at[table_ref[where_ref[0]]], out_ref, sem)
    copy.start()
    copy.wait()


def pick_columns(where_ref, tokens_ref, after_ref, out_ref, sem):
    rows = after_ref.shape[0]
    other = 1 - where_ref[1]
    copies = []
    for block in range(out_ref.shape[1] // rows):
        start = pl.multiple_of((2 * block + other) * rows, 128)
        copies.append(
            pltpu.make_async_copy(
                tokens_ref.at[0, :, pl.ds(start, rows)],
                out_ref.at[:, pl.ds(block * rows, rows)],
                sem.at[block],
            )
        )
    for copy in copies:
        copy.start()
    for copy in copies:
        copy.wait()


def products(where_ref, tokens_ref, taken_ref, weights_ref, block):
    rows = weights_ref.shape[0]
    own = pl.multiple_of((2 * block + where_ref[1]) * rows, 128)
    lent = pl.multiple_of(block * rows, 128)
    weights = weights_ref[...]
    return (
        jnp.dot(tokens_ref[0, :, pl.ds(own, rows)], weights, preferred_element_type=jnp.float32),
        jnp.dot(taken_ref[:, pl.ds(lent, rows)], weights, preferred_element_type=jnp.float32),
    )


def first_products(where_ref, tokens_ref, taken_ref, weights_ref, out_ref, turned_ref):
    rows, tok = weights_ref.shape[0], taken_ref.shape[0]
    a, b = products(where_ref, tokens_ref, taken_ref, weights_ref, where_ref[2])
    out_ref[:tok] = a
    out_ref[tok:] = b
    for block in range(turned_ref.shape[0] // rows):
        own = pl.multiple_of((2 * block + where_ref[1]) * rows, 128)
        spot = pl.ds(block * rows, rows)
        turned_ref[spot, :tok] = tokens_ref[0, :, pl.ds(own, rows)].T
        turned_ref[spot, tok:] = taken_ref[:, spot].T


def next_products(step, where_ref, tokens_ref, taken_ref, weights_ref, sum_ref, out_ref):
    tok = taken_ref.shape[0]
    chips = taken_ref.shape[1] // weights_ref.shape[0]
    block = lax.rem(where_ref[2] + chips - step, chips)
    a, b = products(where_ref, tokens_ref, taken_ref, weights_ref, block)
    out_ref[:tok] = sum_ref[:tok] + a
    out_ref[tok:] = sum_ref[tok:] + b


def cotangent_of(latent, upstream):
    inverse_rms = lax.rsqrt(jnp.mean(latent * latent, axis=-1, keepdims=True) + 1e-06)
    normed = latent * inverse_rms
    return (
        inverse_rms * (upstream - normed * jnp.mean(upstream * normed, axis=-1, keepdims=True))
    ).astype(jnp.bfloat16)


def sent_gradients(where_ref, mine_ref, other_ref, up_ref, other_up_ref, turned_ref, *outs):
    latent_ref, outs = outs[0], outs[1:]
    tok = up_ref.shape[0]
    latent_ref[:tok] = cotangent_of(
        mine_ref[:tok] + other_ref[tok:], up_ref[...].astype(jnp.float32)
    )
    latent_ref[tok:] = cotangent_of(
        mine_ref[tok:] + other_ref[:tok], other_up_ref[...].astype(jnp.float32)
    )
    part = outs[0].shape[0] if outs else 0
    chips = len(outs) // CHAINS + 1
    for i, out_ref in enumerate(outs):
        block = lax.rem(where_ref[2] + 1 + i // CHAINS, chips)
        start = pl.multiple_of(block * part * CHAINS + (i % CHAINS) * part, 16)
        out_ref[...] = jnp.dot(
            turned_ref[pl.ds(start, part), :], latent_ref[...], preferred_element_type=jnp.float32
        ).astype(out_ref.dtype)


def kept_gradients(where_ref, turned_ref, latent_ref, *outs):
    part = outs[0].shape[0]
    for i, out_ref in enumerate(outs):
        start = pl.multiple_of(where_ref[2] * part * CHAINS + i * part, 16)
        out_ref[...] = jnp.dot(
            turned_ref[pl.ds(start, part), :], latent_ref[...], preferred_element_type=jnp.float32
        )


def apply_blocks(steps, table_ref, source_ref, where_ref, weights_ref, moment_ref, *refs):
    count = len(steps)
    blocks, rest = refs[:count], refs[count:]
    out_weights, out_moment, new_weights, new_moment, sems = rest
    paths = table_ref.shape[0]
    tile = 64
    copies = []
    for i, (step, start) in enumerate(steps):
        module = table_ref[source_ref[(where_ref[0] * 2 + where_ref[1]) * paths + step]]
        rows = blocks[i].shape[0]

        def work(t, _, i=i, step=step, start=start, module=module):
            here = pl.ds(pl.multiple_of(t * tile, tile), tile)
            spot = pl.ds(pl.multiple_of(start + t * tile, tile), tile)
            a, b = outer_update(
                weights_ref[module, spot],
                moment_ref[module, spot],
                blocks[i][here].astype(jnp.float32),
            )
            new_weights[step, spot] = a
            new_moment[step, spot] = b
            return 0

        lax.fori_loop(0, rows // tile, work, 0)
        span = pl.ds(start, rows)
        for k, (src, dst) in enumerate(((new_weights, out_weights), (new_moment, out_moment))):
            copy = pltpu.make_async_copy(src.at[step, span], dst.at[module, span], sems.at[i, k])
            copy.start()
            copies.append(copy)
    for copy in copies:
        copy.wait()


def body(tokens, cotangent, module_table, module_weights, momentum):
    paths, shards = lax.axis_size("path"), lax.axis_size("fsdp")
    chips = shards // 2
    path_id, shard_id = lax.axis_index("path"), lax.axis_index("fsdp")
    tok_rows, width = tokens.shape[1:]
    module_count, rows, features = module_weights.shape
    step_size = math.sqrt(width / (tok_rows * shards))
    table = module_table[:, 0]
    where = jnp.stack([path_id, shard_id & 1, shard_id >> 1]).astype(jnp.int32)
    f32, bf16 = jnp.float32, jnp.bfloat16
    shape = jax.ShapeDtypeStruct
    dma = pltpu.SemaphoreType.DMA

    to_core = [(i, i ^ 1) for i in range(shards)]

    def to_chip(step):
        return [(i, (i + 2 * step) % shards) for i in range(shards)]

    own_weights = call(
        pick_rows, shape((rows, features), bf16), [SMEM, SMEM, ANY], VMEM,
        (table, where, module_weights), [dma],
    )
    lent_weights = [lax.ppermute(own_weights, "fsdp", to_chip(s)) for s in range(1, chips)]
    given = call(
        pick_columns, shape((tok_rows, chips * rows), bf16), [SMEM, ANY, ANY], VMEM,
        (where, tokens, own_weights), [dma((chips,))],
    )
    taken = lax.ppermute(given, "fsdp", to_core)
    other_up = lax.ppermute(cotangent[0], "fsdp", to_core)
    partial, turned = call(
        first_products,
        [shape((2 * tok_rows, features), f32), shape((chips * rows, 2 * tok_rows), bf16)],
        [SMEM] + [VMEM] * 3, [VMEM] * 2, (where, tokens, taken, own_weights),
    )
    for s in range(1, chips):
        partial = call(
            functools.partial(next_products, s), shape(partial.shape, f32),
            [SMEM] + [VMEM] * 4, VMEM, (where, tokens, taken, lent_weights[s - 1], partial),
        )
    other = lax.ppermute(partial, "fsdp", to_core)
    part = rows // CHAINS
    latent_cotangent, *sent = call(
        sent_gradients,
        [shape((2 * tok_rows, features), bf16)]
        + [shape((part, features), bf16)] * (CHAINS * (chips - 1)),
        [SMEM] + [VMEM] * 5, [VMEM] * (1 + CHAINS * (chips - 1)),
        (where, partial, other, cotangent[0], other_up, turned),
    )
    kept = call(
        kept_gradients, [shape((part, features), f32)] * CHAINS,
        [SMEM] + [VMEM] * 2, [VMEM] * CHAINS, (where, turned, latent_cotangent),
    )
    held = []
    for c in range(CHAINS):
        total = kept[c]
        for s in range(1, chips):
            arrived = lax.ppermute(sent[(s - 1) * CHAINS + c], "fsdp", to_chip(s))
            total = total + arrived.astype(f32)
        held.append(total * step_size)

    if paths != module_count:
        module = lax.dynamic_index_in_dim(table, path_id, 0, keepdims=False)
        module_ids = jnp.arange(module_count, dtype=jnp.int32)
        picked = (module_ids == module).astype(f32)
        counts = jnp.sum((table[:, None] == module_ids[None, :]).astype(f32), axis=0)
        summed = lax.psum(picked[:, None, None] * jnp.concatenate(held)[None], "path")
        return outer_update(module_weights, momentum, summed / counts[:, None, None])

    pairs, source = ring_plan(paths, shards)
    held = [h.astype(bf16) for h in held]
    blocks, steps = [], []
    for step in range(paths):
        for c in range(CHAINS):
            blocks.append(held[c])
            steps.append((step, c * part))
            if step < paths - 1:
                held[c] = lax.ppermute(held[c], ("path", "fsdp"), pairs)
    return call(
        functools.partial(apply_blocks, steps),
        [shape(module_weights.shape, bf16), shape(momentum.shape, f32)],
        [SMEM] * 3 + [VMEM] * (2 + len(blocks)), [ANY] * 2,
        (table, jnp.asarray(source.reshape(-1)), where, module_weights, momentum, *blocks),
        [
            pltpu.VMEM(module_weights.shape, bf16),
            pltpu.VMEM(momentum.shape, f32),
            dma((len(blocks), 2)),
        ],
        limit=16,
    )


def solution(mesh):
    return jax.shard_map(
        body,
        mesh=mesh,
        in_specs=(
            P("path", "fsdp", None),
            P("path", "fsdp", None),
            P(),
            P(None, "fsdp", None),
            P(None, "fsdp", None),
        ),
        out_specs=(P(None, "fsdp", None), P(None, "fsdp", None)),
        check_vma=False,
    )
```

```python
import functools
import math

import jax
import jax.numpy as jnp
from jax import lax
from jax.experimental import pallas as pl
from jax.experimental.pallas import tpu as pltpu
from jax.sharding import PartitionSpec as P

CHAINS = 2
PIECES = 4
MIB = 1 << 20
VMEM = pl.BlockSpec(memory_space=pltpu.VMEM)
SMEM = pl.BlockSpec(memory_space=pltpu.SMEM)
HBM = pl.BlockSpec(memory_space=pltpu.HBM)


def outer_update(weights, moment, average):
    new_moment = 0.9 * moment + average
    new_weights = (weights.astype(jnp.float32) - 0.7 * (average + 0.9 * new_moment)).astype(
        jnp.bfloat16
    )
    return (new_weights, new_moment)


def ring_order(paths):
    return [p for p in range(0, paths, 2)] + [p for p in range(paths - 1, 0, -2)]


def modules_on_ring(table, path_id):
    paths = table.shape[0]
    ids = jnp.arange(paths, dtype=jnp.int32)
    order = jnp.asarray(ring_order(paths), jnp.int32)
    place = jnp.sum(jnp.where(order == path_id, ids, 0))
    there = (ids + ids[:, None, None]) % paths == place
    on_ring = jnp.sum(jnp.where(there, order, 0), axis=-1, keepdims=True)[:, 0]
    modules = jnp.max(jnp.where(on_ring == ids, table, 0), axis=-1, keepdims=True)
    return jnp.broadcast_to(modules, (paths, 128)).astype(jnp.int32)


def ring_pairs(paths):
    order = ring_order(paths)
    place = {p: i for i, p in enumerate(order)}
    return {way: [(p, order[(place[p] + way) % paths]) for p in range(paths)] for way in (1, -1)}


def cuts(rows):
    unit = next(u for u in (64, 32, 16, 1) if rows % u == 0 and rows >= u * CHAINS)
    share, more = divmod(rows // unit, CHAINS)
    sizes = [unit * (share + (c < more)) for c in range(CHAINS)]
    return [(sum(sizes[:c]), size) for c, size in enumerate(sizes)]


def call(
    kernel, out_shape, in_specs, out_specs, args, scratch=(), limit=8, traffic=0, aliases=None
):
    return pl.pallas_call(
        kernel,
        in_specs=in_specs,
        out_specs=out_specs,
        out_shape=out_shape,
        scratch_shapes=list(scratch),
        compiler_params=pltpu.CompilerParams(vmem_limit_bytes=limit * MIB),
        cost_estimate=pl.CostEstimate(flops=0, bytes_accessed=traffic, transcendentals=0),
        input_output_aliases=aliases or {},
        name=kernel.func.__name__ if isinstance(kernel, functools.partial) else kernel.__name__,
    )(*args)


def core_and_chip():
    shard = lax.axis_index("fsdp")
    return shard & 1, shard >> 1


def pick_rows(table_ref, weights_ref, out_ref, sem):
    module = table_ref[lax.axis_index("path")]
    copy = pltpu.make_async_copy(weights_ref.at[module], out_ref, sem)
    copy.start()
    copy.wait()


def pick_columns(tokens_ref, after_ref, *refs):
    outs, sem = refs[:-1], refs[-1]
    rows = after_ref.shape[0]
    core, _ = core_and_chip()
    copies = []
    for i, out_ref in enumerate(outs):
        part = out_ref.shape[0]
        for block in range(out_ref.shape[1] // rows):
            start = pl.multiple_of((2 * block + 1 - core) * rows, 128)
            copies.append(
                pltpu.make_async_copy(
                    tokens_ref.at[0, pl.ds(i * part, part), pl.ds(start, rows)],
                    out_ref.at[:, pl.ds(block * rows, rows)],
                    sem.at[i, block],
                )
            )
    for copy in copies:
        copy.start()
    for copy in copies:
        copy.wait()


def products(tokens_ref, taken_ref, weights_ref, block):
    rows = weights_ref.shape[0]
    core, _ = core_and_chip()
    own = pl.multiple_of((2 * block + core) * rows, 128)
    lent = pl.multiple_of(block * rows, 128)
    weights = weights_ref[...]
    return (
        jnp.dot(tokens_ref[0, :, pl.ds(own, rows)], weights, preferred_element_type=jnp.float32),
        jnp.dot(taken_ref[:, pl.ds(lent, rows)], weights, preferred_element_type=jnp.float32),
    )


def first_products(tokens_ref, weights_ref, *refs):
    pieces, (out_ref, turned_ref, taken_ref) = refs[:-3], refs[-3:]
    rows, tok = weights_ref.shape[0], taken_ref.shape[0]
    part = pieces[0].shape[0]
    for i, piece in enumerate(pieces):
        taken_ref[i * part : (i + 1) * part] = piece[...]
    core, chip = core_and_chip()
    a, b = products(tokens_ref, taken_ref, weights_ref, chip)
    out_ref[:tok] = a
    out_ref[tok:] = b
    for block in range(turned_ref.shape[0] // rows):
        own = pl.multiple_of((2 * block + core) * rows, 128)
        spot = pl.ds(block * rows, rows)
        turned_ref[spot, :tok] = tokens_ref[0, :, pl.ds(own, rows)].T
        turned_ref[spot, tok:] = taken_ref[:, spot].T


def next_products(step, tokens_ref, taken_ref, weights_ref, sum_ref, out_ref):
    tok = taken_ref.shape[0]
    chips = taken_ref.shape[1] // weights_ref.shape[0]
    block = lax.rem(core_and_chip()[1] + chips - step, chips)
    a, b = products(tokens_ref, taken_ref, weights_ref, block)
    out_ref[:tok] = sum_ref[:tok] + a
    out_ref[tok:] = sum_ref[tok:] + b


def cotangent_of(latent, upstream):
    inverse_rms = lax.rsqrt(jnp.mean(latent * latent, axis=-1, keepdims=True) + 1e-06)
    normed = latent * inverse_rms
    return (
        inverse_rms * (upstream - normed * jnp.mean(upstream * normed, axis=-1, keepdims=True))
    ).astype(jnp.bfloat16)


def sent_gradients(mine_ref, other_ref, up_ref, other_up_ref, turned_ref, *outs):
    latent_ref, outs = outs[0], outs[1:]
    tok = up_ref.shape[0]
    latent_ref[:tok] = cotangent_of(
        mine_ref[:tok] + other_ref[tok:], up_ref[...].astype(jnp.float32)
    )
    latent_ref[tok:] = cotangent_of(
        mine_ref[tok:] + other_ref[:tok], other_up_ref[...].astype(jnp.float32)
    )
    chips = len(outs) // CHAINS + 1
    rows = turned_ref.shape[0] // chips
    for i, out_ref in enumerate(outs):
        block = lax.rem(core_and_chip()[1] + 1 + i // CHAINS, chips)
        offset, size = cuts(rows)[i % CHAINS]
        start = pl.multiple_of(block * rows + offset, 16)
        out_ref[...] = jnp.dot(
            turned_ref[pl.ds(start, size), :], latent_ref[...], preferred_element_type=jnp.float32
        ).astype(out_ref.dtype)


def kept_gradients(turned_ref, latent_ref, *outs):
    rows = sum(out_ref.shape[0] for out_ref in outs)
    for out_ref, (offset, size) in zip(outs, cuts(rows), strict=True):
        start = pl.multiple_of(core_and_chip()[1] * rows + offset, 16)
        out_ref[...] = jnp.dot(
            turned_ref[pl.ds(start, size), :], latent_ref[...], preferred_element_type=jnp.float32
        )


def apply_blocks(steps, modules_ref, weights_ref, moment_ref, *refs):
    blocks, rest = refs[: len(steps)], refs[-5:]
    out_weights, out_moment, new_weights, new_moment, sems = rest
    copies = []
    for i, (behind, start) in enumerate(steps):
        module = jnp.max(modules_ref[behind : behind + 1, :])
        rows = blocks[i].shape[0]
        tile = math.gcd(rows, 64)

        def work(t, _, i=i, start=start, module=module, tile=tile):
            here = pl.ds(pl.multiple_of(t * tile, tile), tile)
            spot = pl.ds(pl.multiple_of(start + t * tile, tile), tile)
            a, b = outer_update(
                weights_ref[module, spot],
                moment_ref[module, spot],
                blocks[i][here].astype(jnp.float32),
            )
            new_weights[i, here] = a
            new_moment[i, here] = b
            return 0

        lax.fori_loop(0, rows // tile, work, 0)
        here, spot = pl.ds(0, rows), pl.ds(start, rows)
        for k, (src, dst) in enumerate(((new_weights, out_weights), (new_moment, out_moment))):
            copy = pltpu.make_async_copy(src.at[i, here], dst.at[module, spot], sems.at[i, k])
            copy.start()
            copies.append(copy)
    for copy in copies:
        copy.wait()


def body(tokens, cotangent, module_table, module_weights, momentum):
    paths, shards = lax.axis_size("path"), lax.axis_size("fsdp")
    chips = shards // 2
    path_id = lax.axis_index("path")
    tok_rows, width = tokens.shape[1:]
    module_count, rows, features = module_weights.shape
    step_size = math.sqrt(width / (tok_rows * shards))
    table = module_table[:, 0]
    f32, bf16 = jnp.float32, jnp.bfloat16
    shape = jax.ShapeDtypeStruct
    dma = pltpu.SemaphoreType.DMA

    to_core = [(i, i ^ 1) for i in range(shards)]

    def to_chip(step):
        return [(i, (i + 2 * step) % shards) for i in range(shards)]

    own_weights = call(
        pick_rows, shape((rows, features), bf16), [SMEM, HBM], VMEM,
        (table, module_weights), [dma], limit=50,
    )
    lent_weights = [lax.ppermute(own_weights, "fsdp", to_chip(s)) for s in range(1, chips)]
    pieces = [shape((tok_rows // PIECES, chips * rows), bf16)] * PIECES
    given = call(
        pick_columns, pieces, [HBM, VMEM], [VMEM] * PIECES,
        (tokens, own_weights), [dma((PIECES, chips))],
    )
    taken = [lax.ppermute(g, "fsdp", to_core) for g in given]
    other_up = lax.ppermute(cotangent[0], "fsdp", to_core)
    partial, turned, taken = call(
        first_products,
        [
            shape((2 * tok_rows, features), f32),
            shape((chips * rows, 2 * tok_rows), bf16),
            shape((tok_rows, chips * rows), bf16),
        ],
        [VMEM] * (2 + PIECES), [VMEM] * 3, (tokens, own_weights, *taken),
    )
    modules = modules_on_ring(table, path_id)
    partial, modules = lax.optimization_barrier((partial, modules))
    for s in range(1, chips):
        partial = call(
            functools.partial(next_products, s), shape(partial.shape, f32),
            [VMEM] * 4, VMEM, (tokens, taken, lent_weights[s - 1], partial),
        )
    other = lax.ppermute(partial, "fsdp", to_core)
    chains = cuts(rows)
    parts = [(size, features) for _, size in chains]
    latent_cotangent, *sent = call(
        sent_gradients,
        [shape((2 * tok_rows, features), bf16)]
        + [shape(p, bf16) for p in parts] * (chips - 1),
        [VMEM] * 5, [VMEM] * (1 + CHAINS * (chips - 1)),
        (partial, other, cotangent[0], other_up, turned),
    )
    kept = call(
        kept_gradients, [shape(p, f32) for p in parts],
        [VMEM] * 2, [VMEM] * CHAINS, (turned, latent_cotangent),
    )
    held = []
    for c in range(CHAINS):
        total = kept[c]
        for s in range(1, chips):
            arrived = lax.ppermute(sent[(s - 1) * CHAINS + c], "fsdp", to_chip(s))
            total = total + arrived.astype(f32)
        held.append(total * step_size)

    if paths != module_count:
        module = lax.dynamic_index_in_dim(table, path_id, 0, keepdims=False)
        module_ids = jnp.arange(module_count, dtype=jnp.int32)
        picked = (module_ids == module).astype(f32)
        counts = jnp.sum((table[:, None] == module_ids[None, :]).astype(f32), axis=0)
        summed = lax.psum(picked[:, None, None] * jnp.concatenate(held)[None], "path")
        return outer_update(module_weights, momentum, summed / counts[:, None, None])

    pairs = ring_pairs(paths)
    outs = []

    def apply(group, outs):
        steps = [(behind, start) for behind, start, _ in group]
        blocks = [block for _, _, block in group]
        most = (len(group), max(block.shape[0] for block in blocks), features)
        return call(
            functools.partial(apply_blocks, steps),
            [shape(module_weights.shape, bf16), shape(momentum.shape, f32)],
            [VMEM] * (3 + len(blocks)) + [HBM] * len(outs), [HBM] * 2,
            (modules, module_weights, momentum, *blocks, *outs),
            [pltpu.VMEM(most, bf16), pltpu.VMEM(most, f32), dma((len(blocks), 2))],
            limit=16,
            traffic=8 * sum(block.size for block in blocks),
            aliases={3 + len(blocks) + i: i for i in range(len(outs))},
        )

    held = [h.astype(bf16) for h in held]
    group = [(0, chains[c][0], h) for c, h in enumerate(held)]
    moving = [[h, h] for h in held]
    waiting = [[(0, start, h)] for (start, _), h in zip(chains, held)]
    for step in range(1, paths // 2 + 1):
        last = 2 * step == paths
        for c, (start, size) in enumerate(chains):
            pair, starts = moving[c], [start, start]
            if last:
                pair = [pair[0][: size // 2], pair[1][size // 2 :]]
                starts = [start, start + size // 2]
            if step > 2 and c == 0:
                pair, outs = lax.optimization_barrier((pair, outs))
            else:
                pair = lax.optimization_barrier(tuple(pair))
            moving[c] = [lax.ppermute(b, "path", pairs[way]) for b, way in zip(pair, (1, -1))]
            if step > 1 and c == 0:
                outs = apply([one for group in waiting for one in group], outs)
                waiting = [[] for _ in chains]
            waiting[c] += [
                ((way * step) % paths, first, b)
                for b, first, way in zip(moving[c], starts, (1, -1))
            ]
    for group in waiting:
        outs = apply(group, outs)
    return tuple(outs)


def solution(mesh):
    return jax.shard_map(
        body,
        mesh=mesh,
        in_specs=(
            P("path", "fsdp", None),
            P("path", "fsdp", None),
            P(),
            P(None, "fsdp", None),
            P(None, "fsdp", None),
        ),
        out_specs=(P(None, "fsdp", None), P(None, "fsdp", None)),
        check_vma=False,
    )
```

```python
import functools
import math

import jax
import jax.numpy as jnp
from jax import lax
from jax.experimental import pallas as pl
from jax.experimental.pallas import tpu as pltpu
from jax.sharding import PartitionSpec as P

CHAINS = 2
PIECES = 4
MIB = 1 << 20
VMEM = pl.BlockSpec(memory_space=pltpu.VMEM)
SMEM = pl.BlockSpec(memory_space=pltpu.SMEM)
HBM = pl.BlockSpec(memory_space=pltpu.HBM)


def outer_update(weights, moment, average):
    new_moment = 0.9 * moment + average
    new_weights = (weights.astype(jnp.float32) - 0.7 * (average + 0.9 * new_moment)).astype(
        jnp.bfloat16
    )
    return (new_weights, new_moment)


def ring_order(paths):
    return [p for p in range(0, paths, 2)] + [p for p in range(paths - 1, 0, -2)]


def modules_on_ring(table, path_id):
    paths = table.shape[0]
    ids = jnp.arange(paths, dtype=jnp.int32)
    order = jnp.asarray(ring_order(paths), jnp.int32)
    place = jnp.sum(jnp.where(order == path_id, ids, 0))
    there = (ids + ids[:, None, None]) % paths == place
    on_ring = jnp.sum(jnp.where(there, order, 0), axis=-1, keepdims=True)[:, 0]
    modules = jnp.max(jnp.where(on_ring == ids, table, 0), axis=-1, keepdims=True)
    return jnp.broadcast_to(modules, (paths, 128)).astype(jnp.int32)


def ring_pairs(paths):
    order = ring_order(paths)
    place = {p: i for i, p in enumerate(order)}
    return {way: [(p, order[(place[p] + way) % paths]) for p in range(paths)] for way in (1, -1)}


def cuts(rows):
    unit = next(u for u in (64, 32, 16, 1) if rows % u == 0 and rows >= u * CHAINS)
    share, more = divmod(rows // unit, CHAINS)
    sizes = [unit * (share + (c < more)) for c in range(CHAINS)]
    return [(sum(sizes[:c]), size) for c, size in enumerate(sizes)]


def far_share(size):
    return size // 2


def call(
    kernel, out_shape, in_specs, out_specs, args, scratch=(), limit=8, traffic=0, aliases=None
):
    return pl.pallas_call(
        kernel,
        in_specs=in_specs,
        out_specs=out_specs,
        out_shape=out_shape,
        scratch_shapes=list(scratch),
        compiler_params=pltpu.CompilerParams(vmem_limit_bytes=limit * MIB),
        cost_estimate=pl.CostEstimate(flops=0, bytes_accessed=traffic, transcendentals=0),
        input_output_aliases=aliases or {},
        name=kernel.func.__name__ if isinstance(kernel, functools.partial) else kernel.__name__,
    )(*args)


def core_and_chip():
    shard = lax.axis_index("fsdp")
    return shard & 1, shard >> 1


def pick_rows(table_ref, weights_ref, out_ref, sem):
    table = table_ref[...]
    here = lax.broadcasted_iota(jnp.int32, table.shape, 1) == lax.axis_index("path")
    module = jnp.max(jnp.where(here, table, 0))
    copy = pltpu.make_async_copy(weights_ref.at[module], out_ref, sem)
    copy.start()
    copy.wait()


def pick_columns(tokens_ref, after_ref, *refs):
    outs, sem = refs[:-1], refs[-1]
    rows = after_ref.shape[0]
    core, _ = core_and_chip()
    copies = []
    for i, out_ref in enumerate(outs):
        part = out_ref.shape[0]
        for block in range(out_ref.shape[1] // rows):
            start = pl.multiple_of((2 * block + 1 - core) * rows, 128)
            copies.append(
                pltpu.make_async_copy(
                    tokens_ref.at[0, pl.ds(i * part, part), pl.ds(start, rows)],
                    out_ref.at[:, pl.ds(block * rows, rows)],
                    sem.at[i, block],
                )
            )
    for copy in copies:
        copy.start()
    for copy in copies:
        copy.wait()


def products(tokens_ref, taken_ref, weights_ref, block):
    rows = weights_ref.shape[0]
    core, _ = core_and_chip()
    own = pl.multiple_of((2 * block + core) * rows, 128)
    lent = pl.multiple_of(block * rows, 128)
    weights = weights_ref[...]
    return (
        jnp.dot(tokens_ref[0, :, pl.ds(own, rows)], weights, preferred_element_type=jnp.float32),
        jnp.dot(taken_ref[:, pl.ds(lent, rows)], weights, preferred_element_type=jnp.float32),
    )


def first_products(tokens_ref, weights_ref, *refs):
    pieces, (out_ref, turned_ref, taken_ref) = refs[:-3], refs[-3:]
    rows, tok = weights_ref.shape[0], taken_ref.shape[0]
    part = pieces[0].shape[0]
    for i, piece in enumerate(pieces):
        taken_ref[i * part : (i + 1) * part] = piece[...]
    core, chip = core_and_chip()
    a, b = products(tokens_ref, taken_ref, weights_ref, chip)
    out_ref[:tok] = a
    out_ref[tok:] = b
    for block in range(turned_ref.shape[0] // rows):
        own = pl.multiple_of((2 * block + core) * rows, 128)
        spot = pl.ds(block * rows, rows)
        turned_ref[spot, :tok] = tokens_ref[0, :, pl.ds(own, rows)].T
        turned_ref[spot, tok:] = taken_ref[:, spot].T


def next_products(step, tokens_ref, taken_ref, weights_ref, sum_ref, out_ref):
    tok = taken_ref.shape[0]
    chips = taken_ref.shape[1] // weights_ref.shape[0]
    block = lax.rem(core_and_chip()[1] + chips - step, chips)
    a, b = products(tokens_ref, taken_ref, weights_ref, block)
    out_ref[:tok] = sum_ref[:tok] + a
    out_ref[tok:] = sum_ref[tok:] + b


def cotangent_of(latent, upstream):
    inverse_rms = lax.rsqrt(jnp.mean(latent * latent, axis=-1, keepdims=True) + 1e-06)
    normed = latent * inverse_rms
    return (
        inverse_rms * (upstream - normed * jnp.mean(upstream * normed, axis=-1, keepdims=True))
    ).astype(jnp.bfloat16)


def part_gradient(ahead, part, turned_ref, latent_ref):
    shards = lax.axis_size("fsdp")
    rows = turned_ref.shape[0] // (shards // 2)
    block = lax.rem(core_and_chip()[1] + ahead, shards // 2)
    offset, size = cuts(rows)[part]
    start = pl.multiple_of(block * rows + offset, 16)
    return jnp.dot(
        turned_ref[pl.ds(start, size), :], latent_ref[...], preferred_element_type=jnp.float32
    )


def first_gradients(
    wanted, mine_ref, other_ref, up_ref, other_up_ref, turned_ref, latent_ref, *outs
):
    tok = up_ref.shape[0]
    latent_ref[:tok] = cotangent_of(
        mine_ref[:tok] + other_ref[tok:].astype(jnp.float32), up_ref[...].astype(jnp.float32)
    )
    latent_ref[tok:] = cotangent_of(
        mine_ref[tok:] + other_ref[:tok].astype(jnp.float32),
        other_up_ref[...].astype(jnp.float32),
    )
    for (ahead, part), out_ref in zip(wanted, outs, strict=True):
        out_ref[...] = part_gradient(ahead, part, turned_ref, latent_ref).astype(out_ref.dtype)


def more_gradients(wanted, turned_ref, latent_ref, *outs):
    for (ahead, part), out_ref in zip(wanted, outs, strict=True):
        out_ref[...] = part_gradient(ahead, part, turned_ref, latent_ref).astype(out_ref.dtype)


def apply_blocks(steps, modules_ref, weights_ref, moment_ref, *refs):
    blocks, rest = refs[: len(steps)], refs[-5:]
    out_weights, out_moment, new_weights, new_moment, sems = rest
    copies = []
    for i, (behind, start) in enumerate(steps):
        module = jnp.max(modules_ref[behind : behind + 1, :])
        rows = blocks[i].shape[0]
        tile = math.gcd(rows, 64)

        def work(t, _, i=i, start=start, module=module, tile=tile):
            here = pl.ds(pl.multiple_of(t * tile, tile), tile)
            spot = pl.ds(pl.multiple_of(start + t * tile, tile), tile)
            a, b = outer_update(
                weights_ref[module, spot],
                moment_ref[module, spot],
                blocks[i][here].astype(jnp.float32),
            )
            new_weights[i, here] = a
            new_moment[i, here] = b
            return 0

        lax.fori_loop(0, rows // tile, work, 0)
        here, spot = pl.ds(0, rows), pl.ds(start, rows)
        for k, (src, dst) in enumerate(((new_weights, out_weights), (new_moment, out_moment))):
            copy = pltpu.make_async_copy(src.at[i, here], dst.at[module, spot], sems.at[i, k])
            copy.start()
            copies.append(copy)
    for copy in copies:
        copy.wait()


def body(tokens, cotangent, module_table, module_weights, momentum):
    paths, shards = lax.axis_size("path"), lax.axis_size("fsdp")
    chips = shards // 2
    path_id = lax.axis_index("path")
    tok_rows, width = tokens.shape[1:]
    module_count, rows, features = module_weights.shape
    step_size = math.sqrt(width / (tok_rows * shards))
    table = module_table[:, 0]
    f32, bf16 = jnp.float32, jnp.bfloat16
    shape = jax.ShapeDtypeStruct
    dma = pltpu.SemaphoreType.DMA

    to_core = [(i, i ^ 1) for i in range(shards)]

    def to_chip(step):
        return [(i, (i + 2 * step) % shards) for i in range(shards)]

    own_weights = call(
        pick_rows, shape((rows, features), bf16), [VMEM, HBM], VMEM,
        (table[None], module_weights), [dma], limit=50,
    )
    lent_weights = [lax.ppermute(own_weights, "fsdp", to_chip(s)) for s in range(1, chips)]
    pieces = [shape((tok_rows // PIECES, chips * rows), bf16)] * PIECES
    given = call(
        pick_columns, pieces, [HBM, VMEM], [VMEM] * PIECES,
        (tokens, own_weights), [dma((PIECES, chips))],
    )
    other_up = lax.ppermute(cotangent[0], "fsdp", to_core)
    taken = [lax.ppermute(g, "fsdp", to_core) for g in given]
    partial, turned, taken = call(
        first_products,
        [
            shape((2 * tok_rows, features), f32),
            shape((chips * rows, 2 * tok_rows), bf16),
            shape((tok_rows, chips * rows), bf16),
        ],
        [VMEM] * (2 + PIECES), [VMEM] * 3, (tokens, own_weights, *taken),
    )
    modules = modules_on_ring(table, path_id)
    partial, modules, other_up = lax.optimization_barrier((partial, modules, other_up))
    for s in range(1, chips):
        partial = call(
            functools.partial(next_products, s), shape(partial.shape, f32),
            [VMEM] * 4, VMEM, (tokens, taken, lent_weights[s - 1], partial),
        )
    other = lax.ppermute(partial.astype(bf16), "fsdp", to_core)
    chains = cuts(rows)

    def outputs(wanted):
        return [shape((chains[c][1], features), bf16 if ahead else f32) for ahead, c in wanted]

    first = [(ahead, 0) for ahead in range(1, chips)]
    more = [(ahead, c) for c in range(1, CHAINS) for ahead in range(1, chips)]
    more += [(0, c) for c in range(CHAINS)]
    latent_cotangent, *early = call(
        functools.partial(first_gradients, first),
        [shape((2 * tok_rows, features), bf16)] + outputs(first),
        [VMEM] * 5, [VMEM] * (1 + len(first)),
        (partial, other, cotangent[0], other_up, turned),
    )
    late = call(
        functools.partial(more_gradients, more), outputs(more),
        [VMEM] * 2, [VMEM] * len(more), (turned, latent_cotangent),
    )
    gradients = dict(zip(first + more, [*early, *late], strict=True))
    held = []
    for c in range(CHAINS):
        total = gradients[0, c]
        for s in range(1, chips):
            total = total + lax.ppermute(gradients[s, c], "fsdp", to_chip(s)).astype(f32)
        held.append(total * step_size)

    if paths != module_count:
        module = lax.dynamic_index_in_dim(table, path_id, 0, keepdims=False)
        module_ids = jnp.arange(module_count, dtype=jnp.int32)
        picked = (module_ids == module).astype(f32)
        counts = jnp.sum((table[:, None] == module_ids[None, :]).astype(f32), axis=0)
        summed = lax.psum(picked[:, None, None] * jnp.concatenate(held)[None], "path")
        return outer_update(module_weights, momentum, summed / counts[:, None, None])

    pairs = ring_pairs(paths)
    outs = []

    def apply(group, outs):
        steps = [(behind, start) for behind, start, _ in group]
        blocks = [block for _, _, block in group]
        most = (len(group), max(block.shape[0] for block in blocks), features)
        return call(
            functools.partial(apply_blocks, steps),
            [shape(module_weights.shape, bf16), shape(momentum.shape, f32)],
            [VMEM] * (3 + len(blocks)) + [HBM] * len(outs), [HBM] * 2,
            (modules, module_weights, momentum, *blocks, *outs),
            [pltpu.VMEM(most, bf16), pltpu.VMEM(most, f32), dma((len(blocks), 2))],
            limit=16,
            traffic=8 * sum(block.size for block in blocks),
            aliases={3 + len(blocks) + i: i for i in range(len(outs))},
        )

    held = [h.astype(bf16) for h in held]
    group = [(0, chains[c][0], h) for c, h in enumerate(held)]
    moving = [[h, h] for h in held]
    waiting = [[(0, start, h)] for (start, _), h in zip(chains, held)]
    for step in range(1, paths // 2 + 1):
        last = 2 * step == paths
        for c, (start, size) in enumerate(chains):
            pair, starts = moving[c], [start, start]
            if last:
                first = far_share(size)
                pair = [pair[0][:first], pair[1][first:]]
                starts = [start, start + first]
            if step > 2 and c == 0:
                pair, outs = lax.optimization_barrier((pair, outs))
            else:
                pair = lax.optimization_barrier(tuple(pair))
            moving[c] = [lax.ppermute(b, "path", pairs[way]) for b, way in zip(pair, (1, -1))]
            if step > 1 and c == 0 and not last:
                outs = apply([one for group in waiting for one in group], outs)
                waiting = [[] for _ in chains]
            waiting[c] += [
                ((way * step) % paths, first, b)
                for b, first, way in zip(moving[c], starts, (1, -1))
            ]
    final = waiting[-1][2:]
    waiting[-1] = waiting[-1][:2]
    outs = apply([one for group in waiting for one in group], outs)
    outs = apply(final, outs)
    return tuple(outs)


def solution(mesh):
    return jax.shard_map(
        body,
        mesh=mesh,
        in_specs=(
            P("path", "fsdp", None),
            P("path", "fsdp", None),
            P(),
            P(None, "fsdp", None),
            P(None, "fsdp", None),
        ),
        out_specs=(P(None, "fsdp", None), P(None, "fsdp", None)),
        check_vma=False,
    )
```

```python
import functools
import math

import jax
import jax.numpy as jnp
from jax import lax
from jax.experimental import pallas as pl
from jax.experimental.pallas import tpu as pltpu
from jax.sharding import PartitionSpec as P

CHAINS = 2
PIECES = 4
MIB = 1 << 20
VMEM = pl.BlockSpec(memory_space=pltpu.VMEM)
SMEM = pl.BlockSpec(memory_space=pltpu.SMEM)
HBM = pl.BlockSpec(memory_space=pltpu.HBM)


def outer_update(weights, moment, average):
    new_moment = 0.9 * moment + average
    new_weights = (weights.astype(jnp.float32) - 0.7 * (average + 0.9 * new_moment)).astype(
        jnp.bfloat16
    )
    return (new_weights, new_moment)


def ring_order(paths):
    return [p for p in range(0, paths, 2)] + [p for p in range(paths - 1, 0, -2)]


def modules_on_ring(table, path_id):
    paths = table.shape[0]
    ids = jnp.arange(paths, dtype=jnp.int32)
    order = jnp.asarray(ring_order(paths), jnp.int32)
    place = jnp.sum(jnp.where(order == path_id, ids, 0))
    there = (ids + ids[:, None, None]) % paths == place
    on_ring = jnp.sum(jnp.where(there, order, 0), axis=-1, keepdims=True)[:, 0]
    modules = jnp.max(jnp.where(on_ring == ids, table, 0), axis=-1, keepdims=True)
    return jnp.broadcast_to(modules, (paths, 128)).astype(jnp.int32)


def ring_pairs(paths):
    order = ring_order(paths)
    place = {p: i for i, p in enumerate(order)}
    return {way: [(p, order[(place[p] + way) % paths]) for p in range(paths)] for way in (1, -1)}


def cuts(rows):
    unit = next(u for u in (64, 32, 16, 1) if rows % u == 0 and rows >= u * CHAINS)
    share, more = divmod(rows // unit, CHAINS)
    sizes = [unit * (share + (c < more)) for c in range(CHAINS)]
    return [(sum(sizes[:c]), size) for c, size in enumerate(sizes)]


def far_share(size):
    return size // 2


def call(
    kernel, out_shape, in_specs, out_specs, args, scratch=(), limit=8, traffic=0, aliases=None
):
    return pl.pallas_call(
        kernel,
        in_specs=in_specs,
        out_specs=out_specs,
        out_shape=out_shape,
        scratch_shapes=list(scratch),
        compiler_params=pltpu.CompilerParams(vmem_limit_bytes=limit * MIB),
        cost_estimate=pl.CostEstimate(flops=0, bytes_accessed=traffic, transcendentals=0),
        input_output_aliases=aliases or {},
        name=kernel.func.__name__ if isinstance(kernel, functools.partial) else kernel.__name__,
    )(*args)


def core_and_chip():
    shard = lax.axis_index("fsdp")
    return shard & 1, shard >> 1


def pick_rows(table_ref, weights_ref, out_ref, sem):
    table = table_ref[...]
    here = lax.broadcasted_iota(jnp.int32, table.shape, 1) == lax.axis_index("path")
    module = jnp.max(jnp.where(here, table, 0))
    copy = pltpu.make_async_copy(weights_ref.at[module], out_ref, sem)
    copy.start()
    copy.wait()


def pick_columns(tokens_ref, after_ref, *refs):
    outs, sem = refs[:-1], refs[-1]
    rows = after_ref.shape[0]
    core, _ = core_and_chip()
    copies = []
    for i, out_ref in enumerate(outs):
        part = out_ref.shape[0]
        for block in range(out_ref.shape[1] // rows):
            start = pl.multiple_of((2 * block + 1 - core) * rows, 128)
            copies.append(
                pltpu.make_async_copy(
                    tokens_ref.at[0, pl.ds(i * part, part), pl.ds(start, rows)],
                    out_ref.at[:, pl.ds(block * rows, rows)],
                    sem.at[i, block],
                )
            )
    for copy in copies:
        copy.start()
    for copy in copies:
        copy.wait()


def products(tokens_ref, taken_ref, weights_ref, block):
    rows = weights_ref.shape[0]
    core, _ = core_and_chip()
    own = pl.multiple_of((2 * block + core) * rows, 128)
    lent = pl.multiple_of(block * rows, 128)
    weights = weights_ref[...]
    return (
        jnp.dot(tokens_ref[0, :, pl.ds(own, rows)], weights, preferred_element_type=jnp.float32),
        jnp.dot(taken_ref[:, pl.ds(lent, rows)], weights, preferred_element_type=jnp.float32),
    )


def first_products(tokens_ref, weights_ref, *refs):
    pieces, (out_ref, turned_ref, taken_ref) = refs[:-3], refs[-3:]
    rows, tok = weights_ref.shape[0], taken_ref.shape[0]
    part = pieces[0].shape[0]
    for i, piece in enumerate(pieces):
        taken_ref[i * part : (i + 1) * part] = piece[...]
    core, chip = core_and_chip()
    a, b = products(tokens_ref, taken_ref, weights_ref, chip)
    out_ref[:tok] = a
    out_ref[tok:] = b
    for block in range(turned_ref.shape[0] // rows):
        own = pl.multiple_of((2 * block + core) * rows, 128)
        spot = pl.ds(block * rows, rows)
        turned_ref[spot, :tok] = tokens_ref[0, :, pl.ds(own, rows)].T
        turned_ref[spot, tok:] = taken_ref[:, spot].T


def next_products(step, tokens_ref, taken_ref, weights_ref, sum_ref, out_ref):
    tok = taken_ref.shape[0]
    chips = taken_ref.shape[1] // weights_ref.shape[0]
    block = lax.rem(core_and_chip()[1] + chips - step, chips)
    a, b = products(tokens_ref, taken_ref, weights_ref, block)
    out_ref[:tok] = sum_ref[:tok] + a
    out_ref[tok:] = sum_ref[tok:] + b


def cotangent_of(latent, upstream):
    inverse_rms = lax.rsqrt(jnp.mean(latent * latent, axis=-1, keepdims=True) + 1e-06)
    normed = latent * inverse_rms
    return (
        inverse_rms * (upstream - normed * jnp.mean(upstream * normed, axis=-1, keepdims=True))
    ).astype(jnp.bfloat16)


def part_gradient(ahead, part, turned_ref, latent_ref):
    shards = lax.axis_size("fsdp")
    rows = turned_ref.shape[0] // (shards // 2)
    block = lax.rem(core_and_chip()[1] + ahead, shards // 2)
    offset, size = cuts(rows)[part]
    start = pl.multiple_of(block * rows + offset, 16)
    return jnp.dot(
        turned_ref[pl.ds(start, size), :], latent_ref[...], preferred_element_type=jnp.float32
    )


def first_gradients(
    wanted, mine_ref, other_ref, up_ref, other_up_ref, turned_ref, latent_ref, *outs
):
    tok = up_ref.shape[0]
    latent_ref[:tok] = cotangent_of(
        mine_ref[:tok] + other_ref[tok:].astype(jnp.float32), up_ref[...].astype(jnp.float32)
    )
    latent_ref[tok:] = cotangent_of(
        mine_ref[tok:] + other_ref[:tok].astype(jnp.float32),
        other_up_ref[...].astype(jnp.float32),
    )
    for (ahead, part), out_ref in zip(wanted, outs, strict=True):
        out_ref[...] = part_gradient(ahead, part, turned_ref, latent_ref).astype(out_ref.dtype)


def more_gradients(wanted, turned_ref, latent_ref, *outs):
    for (ahead, part), out_ref in zip(wanted, outs, strict=True):
        out_ref[...] = part_gradient(ahead, part, turned_ref, latent_ref).astype(out_ref.dtype)


def apply_blocks(steps, modules_ref, weights_ref, moment_ref, *refs):
    blocks, rest = refs[: len(steps)], refs[-5:]
    out_weights, out_moment, new_weights, new_moment, sems = rest
    copies = []
    for i, (behind, start) in enumerate(steps):
        module = jnp.max(modules_ref[behind : behind + 1, :])
        rows = blocks[i].shape[0]
        tile = math.gcd(rows, 64)

        def work(t, _, i=i, start=start, module=module, tile=tile):
            here = pl.ds(pl.multiple_of(t * tile, tile), tile)
            spot = pl.ds(pl.multiple_of(start + t * tile, tile), tile)
            a, b = outer_update(
                weights_ref[module, spot],
                moment_ref[module, spot],
                blocks[i][here].astype(jnp.float32),
            )
            new_weights[i, here] = a
            new_moment[i, here] = b
            return 0

        lax.fori_loop(0, rows // tile, work, 0)
        here, spot = pl.ds(0, rows), pl.ds(start, rows)
        for k, (src, dst) in enumerate(((new_weights, out_weights), (new_moment, out_moment))):
            copy = pltpu.make_async_copy(src.at[i, here], dst.at[module, spot], sems.at[i, k])
            copy.start()
            copies.append(copy)
    for copy in copies:
        copy.wait()


def body(tokens, cotangent, module_table, module_weights, momentum):
    paths, shards = lax.axis_size("path"), lax.axis_size("fsdp")
    chips = shards // 2
    path_id = lax.axis_index("path")
    tok_rows, width = tokens.shape[1:]
    module_count, rows, features = module_weights.shape
    step_size = math.sqrt(width / (tok_rows * shards))
    table = module_table[:, 0]
    f32, bf16 = jnp.float32, jnp.bfloat16
    shape = jax.ShapeDtypeStruct
    dma = pltpu.SemaphoreType.DMA

    to_core = [(i, i ^ 1) for i in range(shards)]

    def to_chip(step):
        return [(i, (i + 2 * step) % shards) for i in range(shards)]

    own_weights = call(
        pick_rows, shape((rows, features), bf16), [VMEM, HBM], VMEM,
        (table[None], module_weights), [dma], limit=50,
    )
    lent_weights = [lax.ppermute(own_weights, "fsdp", to_chip(s)) for s in range(1, chips)]
    pieces = [shape((tok_rows // PIECES, chips * rows), bf16)] * PIECES
    given = call(
        pick_columns, pieces, [HBM, VMEM], [VMEM] * PIECES,
        (tokens, own_weights), [dma((PIECES, chips))],
    )
    other_up = lax.ppermute(cotangent[0], "fsdp", to_core)
    taken = [lax.ppermute(g, "fsdp", to_core) for g in given]
    partial, turned, taken = call(
        first_products,
        [
            shape((2 * tok_rows, features), f32),
            shape((chips * rows, 2 * tok_rows), bf16),
            shape((tok_rows, chips * rows), bf16),
        ],
        [VMEM] * (2 + PIECES), [VMEM] * 3, (tokens, own_weights, *taken),
    )
    modules = modules_on_ring(table, path_id)
    partial, modules, other_up = lax.optimization_barrier((partial, modules, other_up))
    for s in range(1, chips):
        partial = call(
            functools.partial(next_products, s), shape(partial.shape, f32),
            [VMEM] * 4, VMEM, (tokens, taken, lent_weights[s - 1], partial),
        )
    other = lax.ppermute(partial.astype(bf16), "fsdp", to_core)
    chains = cuts(rows)

    def outputs(wanted):
        return [shape((chains[c][1], features), bf16 if ahead else f32) for ahead, c in wanted]

    first = [(ahead, 0) for ahead in range(1, chips)]
    more = [(ahead, c) for c in range(1, CHAINS) for ahead in range(1, chips)]
    more += [(0, c) for c in range(CHAINS)]
    latent_cotangent, *early = call(
        functools.partial(first_gradients, first),
        [shape((2 * tok_rows, features), bf16)] + outputs(first),
        [VMEM] * 5, [VMEM] * (1 + len(first)),
        (partial, other, cotangent[0], other_up, turned),
    )
    late = call(
        functools.partial(more_gradients, more), outputs(more),
        [VMEM] * 2, [VMEM] * len(more), (turned, latent_cotangent),
    )
    gradients = dict(zip(first + more, [*early, *late], strict=True))
    held = []
    for c in range(CHAINS):
        total = gradients[0, c]
        for s in range(1, chips):
            total = total + lax.ppermute(gradients[s, c], "fsdp", to_chip(s)).astype(f32)
        held.append(total * step_size)

    if paths != module_count:
        module = lax.dynamic_index_in_dim(table, path_id, 0, keepdims=False)
        module_ids = jnp.arange(module_count, dtype=jnp.int32)
        picked = (module_ids == module).astype(f32)
        counts = jnp.sum((table[:, None] == module_ids[None, :]).astype(f32), axis=0)
        summed = lax.psum(picked[:, None, None] * jnp.concatenate(held)[None], "path")
        return outer_update(module_weights, momentum, summed / counts[:, None, None])

    pairs = ring_pairs(paths)
    outs = []

    def apply(group, outs):
        steps = [(behind, start) for behind, start, _ in group]
        blocks = [block for _, _, block in group]
        most = (len(group), max(block.shape[0] for block in blocks), features)
        return call(
            functools.partial(apply_blocks, steps),
            [shape(module_weights.shape, bf16), shape(momentum.shape, f32)],
            [VMEM] * (3 + len(blocks)) + [HBM] * len(outs), [HBM] * 2,
            (modules, module_weights, momentum, *blocks, *outs),
            [pltpu.VMEM(most, bf16), pltpu.VMEM(most, f32), dma((len(blocks), 2))],
            limit=16,
            traffic=8 * sum(block.size for block in blocks),
            aliases={3 + len(blocks) + i: i for i in range(len(outs))},
        )

    held = [h.astype(bf16) for h in held]
    group = [(0, chains[c][0], h) for c, h in enumerate(held)]
    moving = [[h, h] for h in held]
    waiting = [[(0, start, h)] for (start, _), h in zip(chains, held)]
    for step in range(1, paths // 2 + 1):
        last = 2 * step == paths
        for c, (start, size) in enumerate(chains):
            pair, starts = moving[c], [start, start]
            if last:
                first = far_share(size)
                pair = [pair[0][:first], pair[1][first:]]
                starts = [start, start + first]
            if step > 2 and c == 0:
                pair, outs = lax.optimization_barrier((pair, outs))
            elif not last:
                pair = lax.optimization_barrier(tuple(pair))
            moving[c] = [lax.ppermute(b, "path", pairs[way]) for b, way in zip(pair, (1, -1))]
            if step > 1 and c == 0 and not last:
                outs = apply([one for group in waiting for one in group], outs)
                waiting = [[] for _ in chains]
            waiting[c] += [
                ((way * step) % paths, first, b)
                for b, first, way in zip(moving[c], starts, (1, -1))
            ]
    far = [group[-2:] for group in waiting]
    outs = apply([one for group in waiting for one in group[:-2]], outs)
    for group in far:
        outs = apply(group, outs)
    return tuple(outs)


def solution(mesh):
    return jax.shard_map(
        body,
        mesh=mesh,
        in_specs=(
            P("path", "fsdp", None),
            P("path", "fsdp", None),
            P(),
            P(None, "fsdp", None),
            P(None, "fsdp", None),
        ),
        out_specs=(P(None, "fsdp", None), P(None, "fsdp", None)),
        check_vma=False,
    )
```

```python
import functools
import math

import jax
import jax.numpy as jnp
from jax import lax
from jax.experimental import pallas as pl
from jax.experimental.pallas import tpu as pltpu
from jax.sharding import PartitionSpec as P

CHAINS = 2
PIECES = 4
MIB = 1 << 20
VMEM = pl.BlockSpec(memory_space=pltpu.VMEM)
SMEM = pl.BlockSpec(memory_space=pltpu.SMEM)
HBM = pl.BlockSpec(memory_space=pltpu.HBM)


def outer_update(weights, moment, average):
    new_moment = 0.9 * moment + average
    new_weights = (weights.astype(jnp.float32) - 0.7 * (average + 0.9 * new_moment)).astype(
        jnp.bfloat16
    )
    return (new_weights, new_moment)


def ring_order(paths):
    return [p for p in range(0, paths, 2)] + [p for p in range(paths - 1, 0, -2)]


def modules_on_ring(table, path_id):
    paths = table.shape[0]
    ids = jnp.arange(paths, dtype=jnp.int32)
    order = jnp.asarray(ring_order(paths), jnp.int32)
    place = jnp.sum(jnp.where(order == path_id, ids, 0))
    there = (ids + ids[:, None, None]) % paths == place
    on_ring = jnp.sum(jnp.where(there, order, 0), axis=-1, keepdims=True)[:, 0]
    modules = jnp.max(jnp.where(on_ring == ids, table, 0), axis=-1, keepdims=True)
    return jnp.broadcast_to(modules, (paths, 128)).astype(jnp.int32)


def ring_pairs(paths):
    order = ring_order(paths)
    place = {p: i for i, p in enumerate(order)}
    return {way: [(p, order[(place[p] + way) % paths]) for p in range(paths)] for way in (1, -1)}


def cuts(rows):
    unit = next(u for u in (64, 32, 16, 1) if rows % u == 0 and rows >= u * CHAINS)
    share, more = divmod(rows // unit, CHAINS)
    sizes = [unit * (share + (c < more)) for c in range(CHAINS)]
    return [(sum(sizes[:c]), size) for c, size in enumerate(sizes)]


def call(
    kernel, out_shape, in_specs, out_specs, args, scratch=(), limit=8, traffic=0, aliases=None
):
    return pl.pallas_call(
        kernel,
        in_specs=in_specs,
        out_specs=out_specs,
        out_shape=out_shape,
        scratch_shapes=list(scratch),
        compiler_params=pltpu.CompilerParams(vmem_limit_bytes=limit * MIB),
        cost_estimate=pl.CostEstimate(flops=0, bytes_accessed=traffic, transcendentals=0),
        input_output_aliases=aliases or {},
        name=kernel.func.__name__ if isinstance(kernel, functools.partial) else kernel.__name__,
    )(*args)


def core_and_chip():
    shard = lax.axis_index("fsdp")
    return shard & 1, shard >> 1


def pick_rows(table_ref, weights_ref, out_ref, sem):
    table = table_ref[...]
    here = lax.broadcasted_iota(jnp.int32, table.shape, 1) == lax.axis_index("path")
    module = jnp.max(jnp.where(here, table, 0))
    copy = pltpu.make_async_copy(weights_ref.at[module], out_ref, sem)
    copy.start()
    copy.wait()


def pick_columns(tokens_ref, after_ref, *refs):
    outs, sem = refs[:-1], refs[-1]
    rows = after_ref.shape[0]
    core, _ = core_and_chip()
    copies = []
    for i, out_ref in enumerate(outs):
        part = out_ref.shape[0]
        for block in range(out_ref.shape[1] // rows):
            start = pl.multiple_of((2 * block + 1 - core) * rows, 128)
            copies.append(
                pltpu.make_async_copy(
                    tokens_ref.at[0, pl.ds(i * part, part), pl.ds(start, rows)],
                    out_ref.at[:, pl.ds(block * rows, rows)],
                    sem.at[i, block],
                )
            )
    for copy in copies:
        copy.start()
    for copy in copies:
        copy.wait()


def products(tokens_ref, taken_ref, weights_ref, block):
    rows = weights_ref.shape[0]
    core, _ = core_and_chip()
    own = pl.multiple_of((2 * block + core) * rows, 128)
    lent = pl.multiple_of(block * rows, 128)
    weights = weights_ref[...]
    return (
        jnp.dot(tokens_ref[0, :, pl.ds(own, rows)], weights, preferred_element_type=jnp.float32),
        jnp.dot(taken_ref[:, pl.ds(lent, rows)], weights, preferred_element_type=jnp.float32),
    )


def first_products(tokens_ref, weights_ref, *refs):
    pieces, (out_ref, turned_ref, taken_ref) = refs[:-3], refs[-3:]
    rows, tok = weights_ref.shape[0], taken_ref.shape[0]
    part = pieces[0].shape[0]
    for i, piece in enumerate(pieces):
        taken_ref[i * part : (i + 1) * part] = piece[...]
    core, chip = core_and_chip()
    a, b = products(tokens_ref, taken_ref, weights_ref, chip)
    out_ref[:tok] = a
    out_ref[tok:] = b
    for block in range(turned_ref.shape[0] // rows):
        own = pl.multiple_of((2 * block + core) * rows, 128)
        spot = pl.ds(block * rows, rows)
        turned_ref[spot, :tok] = tokens_ref[0, :, pl.ds(own, rows)].T
        turned_ref[spot, tok:] = taken_ref[:, spot].T


def next_products(step, tokens_ref, taken_ref, weights_ref, sum_ref, out_ref):
    tok = taken_ref.shape[0]
    chips = taken_ref.shape[1] // weights_ref.shape[0]
    block = lax.rem(core_and_chip()[1] + chips - step, chips)
    a, b = products(tokens_ref, taken_ref, weights_ref, block)
    out_ref[:tok] = sum_ref[:tok] + a
    out_ref[tok:] = sum_ref[tok:] + b


def cotangent_of(latent, upstream):
    inverse_rms = lax.rsqrt(jnp.mean(latent * latent, axis=-1, keepdims=True) + 1e-06)
    normed = latent * inverse_rms
    return (
        inverse_rms * (upstream - normed * jnp.mean(upstream * normed, axis=-1, keepdims=True))
    ).astype(jnp.bfloat16)


def part_gradient(ahead, part, turned_ref, latent_ref):
    shards = lax.axis_size("fsdp")
    rows = turned_ref.shape[0] // (shards // 2)
    block = lax.rem(core_and_chip()[1] + ahead, shards // 2)
    offset, size = cuts(rows)[part]
    start = pl.multiple_of(block * rows + offset, 16)
    return jnp.dot(
        turned_ref[pl.ds(start, size), :], latent_ref[...], preferred_element_type=jnp.float32
    )


def first_gradients(
    wanted, mine_ref, other_ref, up_ref, other_up_ref, turned_ref, latent_ref, *outs
):
    tok = up_ref.shape[0]
    latent_ref[:tok] = cotangent_of(
        mine_ref[:tok] + other_ref[tok:].astype(jnp.float32), up_ref[...].astype(jnp.float32)
    )
    latent_ref[tok:] = cotangent_of(
        mine_ref[tok:] + other_ref[:tok].astype(jnp.float32),
        other_up_ref[...].astype(jnp.float32),
    )
    for (ahead, part), out_ref in zip(wanted, outs, strict=True):
        out_ref[...] = part_gradient(ahead, part, turned_ref, latent_ref).astype(out_ref.dtype)


def more_gradients(wanted, turned_ref, latent_ref, *outs):
    for (ahead, part), out_ref in zip(wanted, outs, strict=True):
        out_ref[...] = part_gradient(ahead, part, turned_ref, latent_ref).astype(out_ref.dtype)


def apply_blocks(steps, modules_ref, weights_ref, moment_ref, *refs):
    blocks, rest = refs[: len(steps)], refs[-5:]
    out_weights, out_moment, new_weights, new_moment, sems = rest
    copies = []
    for i, (behind, start) in enumerate(steps):
        module = jnp.max(modules_ref[behind : behind + 1, :])
        rows = blocks[i].shape[0]
        tile = math.gcd(rows, 64)

        def work(t, _, i=i, start=start, module=module, tile=tile):
            here = pl.ds(pl.multiple_of(t * tile, tile), tile)
            spot = pl.ds(pl.multiple_of(start + t * tile, tile), tile)
            a, b = outer_update(
                weights_ref[module, spot],
                moment_ref[module, spot],
                blocks[i][here].astype(jnp.float32),
            )
            new_weights[i, here] = a
            new_moment[i, here] = b
            return 0

        lax.fori_loop(0, rows // tile, work, 0)
        here, spot = pl.ds(0, rows), pl.ds(start, rows)
        for k, (src, dst) in enumerate(((new_weights, out_weights), (new_moment, out_moment))):
            copy = pltpu.make_async_copy(src.at[i, here], dst.at[module, spot], sems.at[i, k])
            copy.start()
            copies.append(copy)
    for copy in copies:
        copy.wait()


def body(tokens, cotangent, module_table, module_weights, momentum):
    paths, shards = lax.axis_size("path"), lax.axis_size("fsdp")
    chips = shards // 2
    path_id = lax.axis_index("path")
    tok_rows, width = tokens.shape[1:]
    module_count, rows, features = module_weights.shape
    step_size = math.sqrt(width / (tok_rows * shards))
    table = module_table[:, 0]
    f32, bf16 = jnp.float32, jnp.bfloat16
    shape = jax.ShapeDtypeStruct
    dma = pltpu.SemaphoreType.DMA

    to_core = [(i, i ^ 1) for i in range(shards)]

    def to_chip(step):
        return [(i, (i + 2 * step) % shards) for i in range(shards)]

    own_weights = call(
        pick_rows, shape((rows, features), bf16), [VMEM, HBM], VMEM,
        (table[None], module_weights), [dma], limit=50,
    )
    lent_weights = [lax.ppermute(own_weights, "fsdp", to_chip(s)) for s in range(1, chips)]
    pieces = [shape((tok_rows // PIECES, chips * rows), bf16)] * PIECES
    given = call(
        pick_columns, pieces, [HBM, VMEM], [VMEM] * PIECES,
        (tokens, own_weights), [dma((PIECES, chips))],
    )
    other_up = lax.ppermute(cotangent[0], "fsdp", to_core)
    taken = [lax.ppermute(g, "fsdp", to_core) for g in given]
    partial, turned, taken = call(
        first_products,
        [
            shape((2 * tok_rows, features), f32),
            shape((chips * rows, 2 * tok_rows), bf16),
            shape((tok_rows, chips * rows), bf16),
        ],
        [VMEM] * (2 + PIECES), [VMEM] * 3, (tokens, own_weights, *taken),
    )
    modules = modules_on_ring(table, path_id)
    partial, modules, other_up = lax.optimization_barrier((partial, modules, other_up))
    for s in range(1, chips):
        partial = call(
            functools.partial(next_products, s), shape(partial.shape, f32),
            [VMEM] * 4, VMEM, (tokens, taken, lent_weights[s - 1], partial),
        )
    other = lax.ppermute(partial.astype(bf16), "fsdp", to_core)
    chains = cuts(rows)

    def outputs(wanted):
        return [shape((chains[c][1], features), bf16 if ahead else f32) for ahead, c in wanted]

    first = [(ahead, 0) for ahead in range(1, chips)]
    more = [(ahead, c) for c in range(1, CHAINS) for ahead in range(1, chips)]
    more += [(0, c) for c in range(CHAINS)]
    latent_cotangent, *early = call(
        functools.partial(first_gradients, first),
        [shape((2 * tok_rows, features), bf16)] + outputs(first),
        [VMEM] * 5, [VMEM] * (1 + len(first)),
        (partial, other, cotangent[0], other_up, turned),
    )
    late = call(
        functools.partial(more_gradients, more), outputs(more),
        [VMEM] * 2, [VMEM] * len(more), (turned, latent_cotangent),
    )
    gradients = dict(zip(first + more, [*early, *late], strict=True))
    held = []
    for c in range(CHAINS):
        total = gradients[0, c]
        for s in range(1, chips):
            total = total + lax.ppermute(gradients[s, c], "fsdp", to_chip(s)).astype(f32)
        held.append(total * step_size)

    if paths != module_count:
        module = lax.dynamic_index_in_dim(table, path_id, 0, keepdims=False)
        module_ids = jnp.arange(module_count, dtype=jnp.int32)
        picked = (module_ids == module).astype(f32)
        counts = jnp.sum((table[:, None] == module_ids[None, :]).astype(f32), axis=0)
        summed = lax.psum(picked[:, None, None] * jnp.concatenate(held)[None], "path")
        return outer_update(module_weights, momentum, summed / counts[:, None, None])

    pairs = ring_pairs(paths)
    outs = []

    def apply(group, outs):
        steps = [(behind, start) for behind, start, _ in group]
        blocks = [block for _, _, block in group]
        most = (len(group), max(block.shape[0] for block in blocks), features)
        return call(
            functools.partial(apply_blocks, steps),
            [shape(module_weights.shape, bf16), shape(momentum.shape, f32)],
            [VMEM] * (3 + len(blocks)) + [HBM] * len(outs), [HBM] * 2,
            (modules, module_weights, momentum, *blocks, *outs),
            [pltpu.VMEM(most, bf16), pltpu.VMEM(most, f32), dma((len(blocks), 2))],
            limit=16,
            traffic=8 * sum(block.size for block in blocks),
            aliases={3 + len(blocks) + i: i for i in range(len(outs))},
        )

    held = [h.astype(bf16) for h in held]
    moving = [[h, h] for h in held]
    waiting = [[(0, start, h)] for (start, _), h in zip(chains, held)]
    for step in range(1, paths // 2 + 1):
        last = 2 * step == paths
        for c, (start, size) in enumerate(chains):
            pair, starts = moving[c], [start, start]
            ways = (1, -1) if c % 2 == 0 else (-1, 1)
            if last:
                pair = [pair[0][: size // 2], pair[1][size // 2 :]]
                starts = [start, start + size // 2]
            if last and c == 0:
                outs = apply(waiting[0], outs)
                waiting[0] = []
            if step > 2 and c == 0:
                pair, outs = lax.optimization_barrier((pair, outs))
            elif not last:
                pair = lax.optimization_barrier(tuple(pair))
            moving[c] = [lax.ppermute(b, "path", pairs[way]) for b, way in zip(pair, ways)]
            if step > 1 and c == 0 and not last:
                outs = apply([one for group in waiting for one in group], outs)
                waiting = [[] for _ in chains]
            waiting[c] += [
                ((way * step) % paths, first, b)
                for b, first, way in zip(moving[c], starts, ways)
            ]
    final = waiting[-1][-2:]
    waiting[-1] = waiting[-1][:-2]
    for group in (waiting[-1], *waiting[:-1], final):
        outs = apply(group, outs)
    return tuple(outs)


def solution(mesh):
    return jax.shard_map(
        body,
        mesh=mesh,
        in_specs=(
            P("path", "fsdp", None),
            P("path", "fsdp", None),
            P(),
            P(None, "fsdp", None),
            P(None, "fsdp", None),
        ),
        out_specs=(P(None, "fsdp", None), P(None, "fsdp", None)),
        check_vma=False,
    )
```

```python
import functools
import math

import jax
import jax.numpy as jnp
from jax import lax
from jax.experimental import pallas as pl
from jax.experimental.pallas import tpu as pltpu
from jax.sharding import PartitionSpec as P

CHAINS = 2
PIECES = 4
MIB = 1 << 20
VMEM = pl.BlockSpec(memory_space=pltpu.VMEM)
SMEM = pl.BlockSpec(memory_space=pltpu.SMEM)
HBM = pl.BlockSpec(memory_space=pltpu.HBM)


def outer_update(weights, moment, average):
    new_moment = 0.9 * moment + average
    new_weights = (weights.astype(jnp.float32) - 0.7 * (average + 0.9 * new_moment)).astype(
        jnp.bfloat16
    )
    return (new_weights, new_moment)


def ring_order(paths):
    return [p for p in range(0, paths, 2)] + [p for p in range(paths - 1, 0, -2)]


def modules_on_ring(table, path_id):
    paths = table.shape[0]
    ids = jnp.arange(paths, dtype=jnp.int32)
    order = jnp.asarray(ring_order(paths), jnp.int32)
    place = jnp.sum(jnp.where(order == path_id, ids, 0))
    there = (ids + ids[:, None, None]) % paths == place
    on_ring = jnp.sum(jnp.where(there, order, 0), axis=-1, keepdims=True)[:, 0]
    modules = jnp.max(jnp.where(on_ring == ids, table, 0), axis=-1, keepdims=True)
    return jnp.broadcast_to(modules, (paths, 128)).astype(jnp.int32)


def ring_pairs(paths):
    order = ring_order(paths)
    place = {p: i for i, p in enumerate(order)}
    return {way: [(p, order[(place[p] + way) % paths]) for p in range(paths)] for way in (1, -1)}


def cuts(rows):
    unit = next(u for u in (64, 32, 16, 1) if rows % u == 0 and rows >= u * CHAINS)
    share, more = divmod(rows // unit, CHAINS)
    sizes = [unit * (share + (c < more)) for c in range(CHAINS)]
    return [(sum(sizes[:c]), size) for c, size in enumerate(sizes)]


def call(
    kernel, out_shape, in_specs, out_specs, args, scratch=(), limit=8, traffic=0, aliases=None
):
    return pl.pallas_call(
        kernel,
        in_specs=in_specs,
        out_specs=out_specs,
        out_shape=out_shape,
        scratch_shapes=list(scratch),
        compiler_params=pltpu.CompilerParams(vmem_limit_bytes=limit * MIB),
        cost_estimate=pl.CostEstimate(flops=0, bytes_accessed=traffic, transcendentals=0),
        input_output_aliases=aliases or {},
        name=kernel.func.__name__ if isinstance(kernel, functools.partial) else kernel.__name__,
    )(*args)


def core_and_chip():
    shard = lax.axis_index("fsdp")
    return shard & 1, shard >> 1


def pick_rows(table_ref, weights_ref, out_ref, sem):
    table = table_ref[...]
    here = lax.broadcasted_iota(jnp.int32, table.shape, 1) == lax.axis_index("path")
    module = jnp.max(jnp.where(here, table, 0))
    copy = pltpu.make_async_copy(weights_ref.at[module], out_ref, sem)
    copy.start()
    copy.wait()


def pick_columns(tokens_ref, after_ref, *refs):
    outs, sem = refs[:-1], refs[-1]
    rows = after_ref.shape[0]
    core, _ = core_and_chip()
    copies = []
    for i, out_ref in enumerate(outs):
        part = out_ref.shape[0]
        for block in range(out_ref.shape[1] // rows):
            start = pl.multiple_of((2 * block + 1 - core) * rows, 128)
            copies.append(
                pltpu.make_async_copy(
                    tokens_ref.at[0, pl.ds(i * part, part), pl.ds(start, rows)],
                    out_ref.at[:, pl.ds(block * rows, rows)],
                    sem.at[i, block],
                )
            )
    for copy in copies:
        copy.start()
    for copy in copies:
        copy.wait()


def products(tokens_ref, taken_ref, weights_ref, block):
    rows = weights_ref.shape[0]
    core, _ = core_and_chip()
    own = pl.multiple_of((2 * block + core) * rows, 128)
    lent = pl.multiple_of(block * rows, 128)
    weights = weights_ref[...]
    return (
        jnp.dot(tokens_ref[0, :, pl.ds(own, rows)], weights, preferred_element_type=jnp.float32),
        jnp.dot(taken_ref[:, pl.ds(lent, rows)], weights, preferred_element_type=jnp.float32),
    )


def first_products(tokens_ref, weights_ref, *refs):
    pieces, (out_ref, turned_ref, taken_ref) = refs[:-3], refs[-3:]
    rows, tok = weights_ref.shape[0], taken_ref.shape[0]
    part = pieces[0].shape[0]
    for i, piece in enumerate(pieces):
        taken_ref[i * part : (i + 1) * part] = piece[...]
    core, chip = core_and_chip()
    a, b = products(tokens_ref, taken_ref, weights_ref, chip)
    out_ref[:tok] = a
    out_ref[tok:] = b
    for block in range(turned_ref.shape[0] // rows):
        own = pl.multiple_of((2 * block + core) * rows, 128)
        spot = pl.ds(block * rows, rows)
        turned_ref[spot, :tok] = tokens_ref[0, :, pl.ds(own, rows)].T
        turned_ref[spot, tok:] = taken_ref[:, spot].T


def next_products(step, tokens_ref, taken_ref, weights_ref, sum_ref, out_ref, rounded_ref):
    tok = taken_ref.shape[0]
    chips = taken_ref.shape[1] // weights_ref.shape[0]
    block = lax.rem(core_and_chip()[1] + chips - step, chips)
    a, b = products(tokens_ref, taken_ref, weights_ref, block)
    a, b = sum_ref[:tok] + a, sum_ref[tok:] + b
    out_ref[:tok] = a
    out_ref[tok:] = b
    rounded_ref[:tok] = a.astype(rounded_ref.dtype)
    rounded_ref[tok:] = b.astype(rounded_ref.dtype)


def cotangent_of(latent, upstream):
    inverse_rms = lax.rsqrt(jnp.mean(latent * latent, axis=-1, keepdims=True) + 1e-06)
    normed = latent * inverse_rms
    return (
        inverse_rms * (upstream - normed * jnp.mean(upstream * normed, axis=-1, keepdims=True))
    ).astype(jnp.bfloat16)


def part_gradient(ahead, part, turned_ref, latent_ref):
    shards = lax.axis_size("fsdp")
    rows = turned_ref.shape[0] // (shards // 2)
    block = lax.rem(core_and_chip()[1] + ahead, shards // 2)
    offset, size = cuts(rows)[part]
    start = pl.multiple_of(block * rows + offset, 16)
    return jnp.dot(
        turned_ref[pl.ds(start, size), :], latent_ref[...], preferred_element_type=jnp.float32
    )


def first_gradients(
    wanted, mine_ref, other_ref, up_ref, other_up_ref, turned_ref, latent_ref, *outs
):
    tok = up_ref.shape[0]
    latent_ref[:tok] = cotangent_of(
        mine_ref[:tok] + other_ref[tok:].astype(jnp.float32), up_ref[...].astype(jnp.float32)
    )
    latent_ref[tok:] = cotangent_of(
        mine_ref[tok:] + other_ref[:tok].astype(jnp.float32),
        other_up_ref[...].astype(jnp.float32),
    )
    for (ahead, part), out_ref in zip(wanted, outs, strict=True):
        out_ref[...] = part_gradient(ahead, part, turned_ref, latent_ref).astype(out_ref.dtype)


def more_gradients(wanted, turned_ref, latent_ref, *outs):
    for (ahead, part), out_ref in zip(wanted, outs, strict=True):
        out_ref[...] = part_gradient(ahead, part, turned_ref, latent_ref).astype(out_ref.dtype)


def apply_blocks(steps, modules_ref, weights_ref, moment_ref, *refs):
    blocks, rest = refs[: len(steps)], refs[-5:]
    out_weights, out_moment, new_weights, new_moment, sems = rest
    copies = []
    for i, (behind, start) in enumerate(steps):
        module = jnp.max(modules_ref[behind : behind + 1, :])
        rows = blocks[i].shape[0]
        tile = math.gcd(rows, 64)

        def work(t, _, i=i, start=start, module=module, tile=tile):
            here = pl.ds(pl.multiple_of(t * tile, tile), tile)
            spot = pl.ds(pl.multiple_of(start + t * tile, tile), tile)
            a, b = outer_update(
                weights_ref[module, spot],
                moment_ref[module, spot],
                blocks[i][here].astype(jnp.float32),
            )
            new_weights[i, here] = a
            new_moment[i, here] = b
            return 0

        lax.fori_loop(0, rows // tile, work, 0)
        here, spot = pl.ds(0, rows), pl.ds(start, rows)
        for k, (src, dst) in enumerate(((new_weights, out_weights), (new_moment, out_moment))):
            copy = pltpu.make_async_copy(src.at[i, here], dst.at[module, spot], sems.at[i, k])
            copy.start()
            copies.append(copy)
    for copy in copies:
        copy.wait()


def body(tokens, cotangent, module_table, module_weights, momentum):
    paths, shards = lax.axis_size("path"), lax.axis_size("fsdp")
    chips = shards // 2
    path_id = lax.axis_index("path")
    tok_rows, width = tokens.shape[1:]
    module_count, rows, features = module_weights.shape
    step_size = math.sqrt(width / (tok_rows * shards))
    table = module_table[:, 0]
    f32, bf16 = jnp.float32, jnp.bfloat16
    shape = jax.ShapeDtypeStruct
    dma = pltpu.SemaphoreType.DMA

    to_core = [(i, i ^ 1) for i in range(shards)]

    def to_chip(step):
        return [(i, (i + 2 * step) % shards) for i in range(shards)]

    own_weights = call(
        pick_rows, shape((rows, features), bf16), [VMEM, HBM], VMEM,
        (table[None], module_weights), [dma], limit=50,
    )
    lent_weights = [lax.ppermute(own_weights, "fsdp", to_chip(s)) for s in range(1, chips)]
    pieces = [shape((tok_rows // PIECES, chips * rows), bf16)] * PIECES
    given = call(
        pick_columns, pieces, [HBM, VMEM], [VMEM] * PIECES,
        (tokens, own_weights), [dma((PIECES, chips))],
    )
    other_up = lax.ppermute(cotangent[0], "fsdp", to_core)
    taken = [lax.ppermute(g, "fsdp", to_core) for g in given]
    partial, turned, taken = call(
        first_products,
        [
            shape((2 * tok_rows, features), f32),
            shape((chips * rows, 2 * tok_rows), bf16),
            shape((tok_rows, chips * rows), bf16),
        ],
        [VMEM] * (2 + PIECES), [VMEM] * 3, (tokens, own_weights, *taken),
    )
    modules = modules_on_ring(table, path_id)
    partial, modules, other_up = lax.optimization_barrier((partial, modules, other_up))
    rounded = partial.astype(bf16)
    for s in range(1, chips):
        partial, rounded = call(
            functools.partial(next_products, s),
            [shape(partial.shape, f32), shape(partial.shape, bf16)],
            [VMEM] * 4, [VMEM] * 2, (tokens, taken, lent_weights[s - 1], partial),
        )
    other = lax.ppermute(rounded, "fsdp", to_core)
    chains = cuts(rows)

    def outputs(wanted):
        return [shape((chains[c][1], features), bf16 if ahead else f32) for ahead, c in wanted]

    first = [(ahead, 0) for ahead in range(1, chips)]
    more = [(ahead, c) for c in range(1, CHAINS) for ahead in range(1, chips)]
    more += [(0, c) for c in range(CHAINS)]
    latent_cotangent, *early = call(
        functools.partial(first_gradients, first),
        [shape((2 * tok_rows, features), bf16)] + outputs(first),
        [VMEM] * 5, [VMEM] * (1 + len(first)),
        (partial, other, cotangent[0], other_up, turned),
    )
    late = call(
        functools.partial(more_gradients, more), outputs(more),
        [VMEM] * 2, [VMEM] * len(more), (turned, latent_cotangent),
    )
    gradients = dict(zip(first + more, [*early, *late], strict=True))
    held = []
    for c in range(CHAINS):
        total = gradients[0, c]
        for s in range(1, chips):
            total = total + lax.ppermute(gradients[s, c], "fsdp", to_chip(s)).astype(f32)
        held.append(total * step_size)

    if paths != module_count:
        module = lax.dynamic_index_in_dim(table, path_id, 0, keepdims=False)
        module_ids = jnp.arange(module_count, dtype=jnp.int32)
        picked = (module_ids == module).astype(f32)
        counts = jnp.sum((table[:, None] == module_ids[None, :]).astype(f32), axis=0)
        summed = lax.psum(picked[:, None, None] * jnp.concatenate(held)[None], "path")
        return outer_update(module_weights, momentum, summed / counts[:, None, None])

    pairs = ring_pairs(paths)
    outs = []

    def apply(group, outs):
        steps = [(behind, start) for behind, start, _ in group]
        blocks = [block for _, _, block in group]
        most = (len(group), max(block.shape[0] for block in blocks), features)
        return call(
            functools.partial(apply_blocks, steps),
            [shape(module_weights.shape, bf16), shape(momentum.shape, f32)],
            [VMEM] * (3 + len(blocks)) + [HBM] * len(outs), [HBM] * 2,
            (modules, module_weights, momentum, *blocks, *outs),
            [pltpu.VMEM(most, bf16), pltpu.VMEM(most, f32), dma((len(blocks), 2))],
            limit=16,
            traffic=8 * sum(block.size for block in blocks),
            aliases={3 + len(blocks) + i: i for i in range(len(outs))},
        )

    held = [h.astype(bf16) for h in held]
    moving = [[h, h] for h in held]
    waiting = [[(0, start, h)] for (start, _), h in zip(chains, held)]
    for step in range(1, paths // 2 + 1):
        last = 2 * step == paths
        for c, (start, size) in enumerate(chains):
            pair, starts = moving[c], [start, start]
            ways = (1, -1) if c % 2 == 0 else (-1, 1)
            if last:
                pair = [pair[0][: size // 2], pair[1][size // 2 :]]
                starts = [start, start + size // 2]
            if last and c == 0:
                outs = apply(waiting[0], outs)
                waiting[0] = []
            if step > 2 and c == 0:
                pair, outs = lax.optimization_barrier((pair, outs))
            elif step < 2:
                pair = lax.optimization_barrier(tuple(pair))
            moving[c] = [lax.ppermute(b, "path", pairs[way]) for b, way in zip(pair, ways)]
            if step > 1 and c == 0 and not last:
                outs = apply([one for group in waiting for one in group], outs)
                waiting = [[] for _ in chains]
            waiting[c] += [
                ((way * step) % paths, first, b)
                for b, first, way in zip(moving[c], starts, ways)
            ]
    final = waiting[-1][-2:]
    waiting[-1] = waiting[-1][:-2]
    for group in (waiting[-1], *waiting[:-1], final):
        outs = apply(group, outs)
    return tuple(outs)


def solution(mesh):
    return jax.shard_map(
        body,
        mesh=mesh,
        in_specs=(
            P("path", "fsdp", None),
            P("path", "fsdp", None),
            P(),
            P(None, "fsdp", None),
            P(None, "fsdp", None),
        ),
        out_specs=(P(None, "fsdp", None), P(None, "fsdp", None)),
        check_vma=False,
    )
```

```python
import functools
import math

import jax
import jax.numpy as jnp
from jax import lax
from jax.experimental import pallas as pl
from jax.experimental.pallas import tpu as pltpu
from jax.sharding import PartitionSpec as P

CHAINS = 2
PIECES = 4
MIB = 1 << 20
VMEM = pl.BlockSpec(memory_space=pltpu.VMEM)
SMEM = pl.BlockSpec(memory_space=pltpu.SMEM)
HBM = pl.BlockSpec(memory_space=pltpu.HBM)


def outer_update(weights, moment, average):
    new_moment = 0.9 * moment + average
    new_weights = (weights.astype(jnp.float32) - 0.7 * (average + 0.9 * new_moment)).astype(
        jnp.bfloat16
    )
    return (new_weights, new_moment)


def ring_order(paths):
    return [p for p in range(0, paths, 2)] + [p for p in range(paths - 1, 0, -2)]


def modules_on_ring(table, path_id):
    paths = table.shape[0]
    ids = jnp.arange(paths, dtype=jnp.int32)
    order = jnp.asarray(ring_order(paths), jnp.int32)
    place = jnp.sum(jnp.where(order == path_id, ids, 0))
    there = (ids + ids[:, None, None]) % paths == place
    on_ring = jnp.sum(jnp.where(there, order, 0), axis=-1, keepdims=True)[:, 0]
    modules = jnp.max(jnp.where(on_ring == ids, table, 0), axis=-1, keepdims=True)
    return jnp.broadcast_to(modules, (paths, 128)).astype(jnp.int32)


def ring_pairs(paths):
    order = ring_order(paths)
    place = {p: i for i, p in enumerate(order)}
    return {way: [(p, order[(place[p] + way) % paths]) for p in range(paths)] for way in (1, -1)}


def cuts(rows):
    unit = next(u for u in (64, 32, 16, 1) if rows % u == 0 and rows >= u * CHAINS)
    share, more = divmod(rows // unit, CHAINS)
    sizes = [unit * (share + (c < more)) for c in range(CHAINS)]
    return [(sum(sizes[:c]), size) for c, size in enumerate(sizes)]


def call(
    kernel, out_shape, in_specs, out_specs, args, scratch=(), limit=8, traffic=0, aliases=None
):
    return pl.pallas_call(
        kernel,
        in_specs=in_specs,
        out_specs=out_specs,
        out_shape=out_shape,
        scratch_shapes=list(scratch),
        compiler_params=pltpu.CompilerParams(vmem_limit_bytes=limit * MIB),
        cost_estimate=pl.CostEstimate(flops=0, bytes_accessed=traffic, transcendentals=0),
        input_output_aliases=aliases or {},
        name=kernel.func.__name__ if isinstance(kernel, functools.partial) else kernel.__name__,
    )(*args)


def core_and_chip():
    shard = lax.axis_index("fsdp")
    return shard & 1, shard >> 1


def pick_rows(table_ref, weights_ref, out_ref, sem):
    table = table_ref[...]
    here = lax.broadcasted_iota(jnp.int32, table.shape, 1) == lax.axis_index("path")
    module = jnp.max(jnp.where(here, table, 0))
    copy = pltpu.make_async_copy(weights_ref.at[module], out_ref, sem)
    copy.start()
    copy.wait()


def pick_columns(tokens_ref, after_ref, *refs):
    outs, sem = refs[:-1], refs[-1]
    rows = after_ref.shape[0]
    core, _ = core_and_chip()
    copies = []
    for i, out_ref in enumerate(outs):
        part = out_ref.shape[0]
        for block in range(out_ref.shape[1] // rows):
            start = pl.multiple_of((2 * block + 1 - core) * rows, 128)
            copies.append(
                pltpu.make_async_copy(
                    tokens_ref.at[0, pl.ds(i * part, part), pl.ds(start, rows)],
                    out_ref.at[:, pl.ds(block * rows, rows)],
                    sem.at[i, block],
                )
            )
    for copy in copies:
        copy.start()
    for copy in copies:
        copy.wait()


def products(tokens_ref, taken_ref, weights_ref, block):
    rows = weights_ref.shape[0]
    core, _ = core_and_chip()
    own = pl.multiple_of((2 * block + core) * rows, 128)
    lent = pl.multiple_of(block * rows, 128)
    weights = weights_ref[...]
    return (
        jnp.dot(tokens_ref[0, :, pl.ds(own, rows)], weights, preferred_element_type=jnp.float32),
        jnp.dot(taken_ref[:, pl.ds(lent, rows)], weights, preferred_element_type=jnp.float32),
    )


def first_products(tokens_ref, weights_ref, *refs):
    pieces, (out_ref, turned_ref, taken_ref) = refs[:-3], refs[-3:]
    rows, tok = weights_ref.shape[0], taken_ref.shape[0]
    part = pieces[0].shape[0]
    for i, piece in enumerate(pieces):
        taken_ref[i * part : (i + 1) * part] = piece[...]
    core, chip = core_and_chip()
    a, b = products(tokens_ref, taken_ref, weights_ref, chip)
    out_ref[:tok] = a
    out_ref[tok:] = b
    for block in range(turned_ref.shape[0] // rows):
        own = pl.multiple_of((2 * block + core) * rows, 128)
        spot = pl.ds(block * rows, rows)
        turned_ref[spot, :tok] = tokens_ref[0, :, pl.ds(own, rows)].T
        turned_ref[spot, tok:] = taken_ref[:, spot].T


def next_products(step, tokens_ref, taken_ref, weights_ref, sum_ref, out_ref, rounded_ref):
    tok = taken_ref.shape[0]
    chips = taken_ref.shape[1] // weights_ref.shape[0]
    block = lax.rem(core_and_chip()[1] + chips - step, chips)
    a, b = products(tokens_ref, taken_ref, weights_ref, block)
    a, b = sum_ref[:tok] + a, sum_ref[tok:] + b
    out_ref[:tok] = a
    out_ref[tok:] = b
    rounded_ref[:tok] = a.astype(rounded_ref.dtype)
    rounded_ref[tok:] = b.astype(rounded_ref.dtype)


def cotangent_of(latent, upstream):
    inverse_rms = lax.rsqrt(jnp.mean(latent * latent, axis=-1, keepdims=True) + 1e-06)
    normed = latent * inverse_rms
    return (
        inverse_rms * (upstream - normed * jnp.mean(upstream * normed, axis=-1, keepdims=True))
    ).astype(jnp.bfloat16)


def part_gradient(ahead, part, turned_ref, latent_ref):
    shards = lax.axis_size("fsdp")
    rows = turned_ref.shape[0] // (shards // 2)
    block = lax.rem(core_and_chip()[1] + ahead, shards // 2)
    offset, size = cuts(rows)[part]
    start = pl.multiple_of(block * rows + offset, 16)
    return jnp.dot(
        turned_ref[pl.ds(start, size), :], latent_ref[...], preferred_element_type=jnp.float32
    )


def first_gradients(
    wanted, mine_ref, other_ref, up_ref, other_up_ref, turned_ref, latent_ref, *outs
):
    tok = up_ref.shape[0]
    latent_ref[:tok] = cotangent_of(
        mine_ref[:tok] + other_ref[tok:].astype(jnp.float32), up_ref[...].astype(jnp.float32)
    )
    latent_ref[tok:] = cotangent_of(
        mine_ref[tok:] + other_ref[:tok].astype(jnp.float32),
        other_up_ref[...].astype(jnp.float32),
    )
    for (ahead, part), out_ref in zip(wanted, outs, strict=True):
        out_ref[...] = part_gradient(ahead, part, turned_ref, latent_ref).astype(out_ref.dtype)


def more_gradients(wanted, turned_ref, latent_ref, *outs):
    for (ahead, part), out_ref in zip(wanted, outs, strict=True):
        out_ref[...] = part_gradient(ahead, part, turned_ref, latent_ref).astype(out_ref.dtype)


def apply_blocks(steps, modules_ref, weights_ref, moment_ref, *refs):
    blocks, rest = refs[: len(steps)], refs[-5:]
    out_weights, out_moment, new_weights, new_moment, sems = rest
    copies = []
    for i, (behind, start) in enumerate(steps):
        module = jnp.max(modules_ref[behind : behind + 1, :])
        rows = blocks[i].shape[0]
        tile = math.gcd(rows, 64)

        def work(t, _, i=i, start=start, module=module, tile=tile):
            here = pl.ds(pl.multiple_of(t * tile, tile), tile)
            spot = pl.ds(pl.multiple_of(start + t * tile, tile), tile)
            a, b = outer_update(
                weights_ref[module, spot],
                moment_ref[module, spot],
                blocks[i][here].astype(jnp.float32),
            )
            new_weights[i, here] = a
            new_moment[i, here] = b
            return 0

        lax.fori_loop(0, rows // tile, work, 0)
        here, spot = pl.ds(0, rows), pl.ds(start, rows)
        for k, (src, dst) in enumerate(((new_moment, out_moment), (new_weights, out_weights))):
            copy = pltpu.make_async_copy(src.at[i, here], dst.at[module, spot], sems.at[i, k])
            copy.start()
            copies.append(copy)
    for copy in copies:
        copy.wait()


def body(tokens, cotangent, module_table, module_weights, momentum):
    paths, shards = lax.axis_size("path"), lax.axis_size("fsdp")
    chips = shards // 2
    path_id = lax.axis_index("path")
    tok_rows, width = tokens.shape[1:]
    module_count, rows, features = module_weights.shape
    step_size = math.sqrt(width / (tok_rows * shards))
    table = module_table[:, 0]
    f32, bf16 = jnp.float32, jnp.bfloat16
    shape = jax.ShapeDtypeStruct
    dma = pltpu.SemaphoreType.DMA

    to_core = [(i, i ^ 1) for i in range(shards)]

    def to_chip(step):
        return [(i, (i + 2 * step) % shards) for i in range(shards)]

    own_weights = call(
        pick_rows, shape((rows, features), bf16), [VMEM, HBM], VMEM,
        (table[None], module_weights), [dma], limit=50,
    )
    lent_weights = [lax.ppermute(own_weights, "fsdp", to_chip(s)) for s in range(1, chips)]
    pieces = [shape((tok_rows // PIECES, chips * rows), bf16)] * PIECES
    given = call(
        pick_columns, pieces, [HBM, VMEM], [VMEM] * PIECES,
        (tokens, own_weights), [dma((PIECES, chips))],
    )
    other_up = lax.ppermute(cotangent[0], "fsdp", to_core)
    taken = [lax.ppermute(g, "fsdp", to_core) for g in given]
    partial, turned, taken = call(
        first_products,
        [
            shape((2 * tok_rows, features), f32),
            shape((chips * rows, 2 * tok_rows), bf16),
            shape((tok_rows, chips * rows), bf16),
        ],
        [VMEM] * (2 + PIECES), [VMEM] * 3, (tokens, own_weights, *taken),
    )
    modules = modules_on_ring(table, path_id)
    partial, modules, other_up = lax.optimization_barrier((partial, modules, other_up))
    rounded = partial.astype(bf16)
    for s in range(1, chips):
        partial, rounded = call(
            functools.partial(next_products, s),
            [shape(partial.shape, f32), shape(partial.shape, bf16)],
            [VMEM] * 4, [VMEM] * 2, (tokens, taken, lent_weights[s - 1], partial),
        )
    other = lax.ppermute(rounded, "fsdp", to_core)
    chains = cuts(rows)

    def outputs(wanted):
        return [shape((chains[c][1], features), bf16 if ahead else f32) for ahead, c in wanted]

    first = [(ahead, 0) for ahead in range(1, chips)]
    more = [(ahead, c) for c in range(1, CHAINS) for ahead in range(1, chips)]
    more += [(0, c) for c in range(CHAINS)]
    latent_cotangent, *early = call(
        functools.partial(first_gradients, first),
        [shape((2 * tok_rows, features), bf16)] + outputs(first),
        [VMEM] * 5, [VMEM] * (1 + len(first)),
        (partial, other, cotangent[0], other_up, turned),
    )
    late = call(
        functools.partial(more_gradients, more), outputs(more),
        [VMEM] * 2, [VMEM] * len(more), (turned, latent_cotangent),
    )
    gradients = dict(zip(first + more, [*early, *late], strict=True))
    held = []
    for c in range(CHAINS):
        total = gradients[0, c]
        for s in range(1, chips):
            total = total + lax.ppermute(gradients[s, c], "fsdp", to_chip(s)).astype(f32)
        held.append(total * step_size)

    if paths != module_count:
        module = lax.dynamic_index_in_dim(table, path_id, 0, keepdims=False)
        module_ids = jnp.arange(module_count, dtype=jnp.int32)
        picked = (module_ids == module).astype(f32)
        counts = jnp.sum((table[:, None] == module_ids[None, :]).astype(f32), axis=0)
        summed = lax.psum(picked[:, None, None] * jnp.concatenate(held)[None], "path")
        return outer_update(module_weights, momentum, summed / counts[:, None, None])

    pairs = ring_pairs(paths)
    outs = []

    def apply(group, outs):
        steps = [(behind, start) for behind, start, _ in group]
        blocks = [block for _, _, block in group]
        most = (len(group), max(block.shape[0] for block in blocks), features)
        return call(
            functools.partial(apply_blocks, steps),
            [shape(module_weights.shape, bf16), shape(momentum.shape, f32)],
            [VMEM] * (3 + len(blocks)) + [HBM] * len(outs), [HBM] * 2,
            (modules, module_weights, momentum, *blocks, *outs),
            [pltpu.VMEM(most, bf16), pltpu.VMEM(most, f32), dma((len(blocks), 2))],
            limit=16,
            traffic=8 * sum(block.size for block in blocks),
            aliases={3 + len(blocks) + i: i for i in range(len(outs))},
        )

    held = [h.astype(bf16) for h in held]
    moving = [[h, h] for h in held]
    waiting = [[(0, start, h)] for (start, _), h in zip(chains, held)]
    for step in range(1, paths // 2 + 1):
        last = 2 * step == paths
        for c, (start, size) in enumerate(chains):
            pair, starts = moving[c], [start, start]
            ways = (1, -1) if c % 2 == 0 else (-1, 1)
            if last:
                pair = [pair[0][: size // 2], pair[1][size // 2 :]]
                starts = [start, start + size // 2]
            if last and c == 0:
                outs = apply(waiting[0], outs)
                waiting[0] = []
            if step > 2 and c == 0:
                pair, outs = lax.optimization_barrier((pair, outs))
            elif step < 2:
                pair = lax.optimization_barrier(tuple(pair))
            moving[c] = [lax.ppermute(b, "path", pairs[way]) for b, way in zip(pair, ways)]
            if step > 1 and c == 0 and not last:
                outs = apply([one for group in waiting for one in group], outs)
                waiting = [[] for _ in chains]
            waiting[c] += [
                ((way * step) % paths, first, b)
                for b, first, way in zip(moving[c], starts, ways)
            ]
    final = waiting[-1][-2:]
    waiting[-1] = waiting[-1][:-2]
    for group in (waiting[-1], *waiting[:-1], final):
        outs = apply(group, outs)
    return tuple(outs)


def solution(mesh):
    return jax.shard_map(
        body,
        mesh=mesh,
        in_specs=(
            P("path", "fsdp", None),
            P("path", "fsdp", None),
            P(),
            P(None, "fsdp", None),
            P(None, "fsdp", None),
        ),
        out_specs=(P(None, "fsdp", None), P(None, "fsdp", None)),
        check_vma=False,
    )
```
